256 devices in a mesh: dp: 8 (over y, core), mem: 32 (over z, x).
Axes of the slice: x: 4, y: 4, z: 8, core: 2. Of those that a mesh axis runs over, the one named last changes fastest.
Arguments:
- slot_weight: bfloat16 [32768, 32], P(('dp', 'mem')), may hold values from -1.1953125 to 1.1953125
- slot_pos: int32 [32768, 32], P(('dp', 'mem')), may hold values from 0 to 1023, as said below
- touched: int32 [256, 32, 32], P(('dp', 'mem')), may hold values from 0 to 255, as said below
- values: bfloat16 [8192, 4096], P('mem'), may hold values from -6 to 6
- cotangent: bfloat16 [32768, 4096], P(('dp', 'mem')), may hold values from -6 to 6
Outputs:
- memory_out: bfloat16 [32768, 4096], P(('dp', 'mem'))
- weight_grad: float32 [32768, 32], P(('dp', 'mem'))
- value_grad: float32 [8192, 4096], P('mem', 'dp')
The draws below stay inside these ranges and needn't reach their ends.
Inputs may be any that keep to these rules, and one draw needn't show every extreme that they name: `slot_pos`: each token's 32 positions are distinct. For each device and owner o, the positions used are o * 32 + j with j below a count c of 1 to 32; in each group of devices along mem, one owner has c = 32 from every device. `touched`: for each device and owner, the entries at the used positions are distinct; entries at unused positions are arbitrary rows.
All inputs are finite; a program needn't handle non-finite values.
Results may differ from the reference program's by a relative error of at most 0.001.
Values may be sent and summed in bfloat16 or wider, within the bound.
No kernel may reach another device: no remote copies, remote signals or barrier semaphores. Data moves between devices by JAX's collectives and lax.ppermute only.
A program may use at most 256 MiB of HBM per device.

```python
import jax
import jax.numpy as jnp
from jax import lax

D = 4096
TOPK = 32
CAP = 32
TOK_DEV = 128
ROWS_DEV = 256
TOKENS = 32768
ROWS = 8192
N_DP = 8
N_MEM = 32


def live_counts(key):
    key = jax.random.fold_in(key, 101)
    key_hot, key_raw, key_full = jax.random.split(key, 3)
    hotness = jax.random.randint(key_hot, (N_DP, 1, N_MEM), 1, 5)
    raw = jax.random.randint(key_raw, (N_DP, N_MEM, N_MEM), 0, CAP)
    least = (TOPK + N_MEM - 1) // N_MEM
    counted = jnp.maximum(1 + raw * hotness // 2, least)
    counted = jnp.minimum(counted, CAP)
    fullest = jax.random.randint(key_full, (N_DP, 1, 1), 0, N_MEM)
    owners = jnp.arange(N_MEM, dtype=jnp.int32)[None, None, :]
    counted = jnp.where(owners == fullest, CAP, counted)
    return counted.reshape(N_DP * N_MEM, N_MEM)


def draw_touched(key, part):
    key = jax.random.fold_in(key, 7)
    spread = 2 ** 30 // ROWS_DEV
    scores = jax.random.randint(key, (N_DP * N_MEM, N_MEM, ROWS_DEV), 0, spread) * ROWS_DEV
    scores = scores + jnp.arange(ROWS_DEV, dtype=jnp.int32)
    _, picked = lax.top_k(scores, CAP)
    return picked.astype(jnp.int32)


def draw_slot_pos(key, part):
    counted = live_counts(key)
    key = jax.random.fold_in(key, 11)
    places = N_MEM * CAP
    within = jnp.arange(CAP, dtype=jnp.int32)[None, None, :]
    valid = (within < counted[:, :, None]).reshape(N_DP * N_MEM, 1, places)
    spread = 2 ** 30 // places
    index = jnp.arange(places, dtype=jnp.int32)
    scores = jax.random.randint(key, (N_DP * N_MEM, TOK_DEV, places), 0, spread) * places + index
    scores = jnp.where(valid, scores, -1 - index)
    _, chosen = lax.top_k(scores, TOPK)
    return chosen.reshape(N_DP * N_MEM * TOK_DEV, TOPK).astype(jnp.int32)


def block_scale(stream_key, shape, pieces, low, high):
    gain, own = 1.0, jax.random.fold_in(stream_key, 6)
    for dim, shards_of in pieces:
        draws = jnp.exp(jax.random.uniform(jax.random.fold_in(own, dim), (shards_of,), jnp.float32, low / len(pieces), high / len(pieces)))
        gain = gain * jnp.repeat(draws, shape[dim] // shards_of).reshape([-1 if axis == dim else 1 for axis in range(len(shape))])
    return gain


def normal_values(own_key, dims, width, most, shards=(), kind=jnp.bfloat16):
    factor_of = block_scale(own_key, dims, shards, -0.22, 0.18) if shards else 1.0
    entries = jax.random.normal(own_key, dims, jnp.float32) * width * factor_of
    return jnp.minimum(jnp.maximum(entries, -most), most).astype(kind)


def setup_inputs(seed: int = 0) -> dict:
    keys = jax.random.split(jax.random.key(seed), 6)
    return {
        "slot_weight": normal_values(keys[0], (TOKENS, TOPK), 0.2, 1.1953125, ((0, 256),)),
        "slot_pos": draw_slot_pos(jax.random.fold_in(keys[5], 71), 0),
        "touched": draw_touched(jax.random.fold_in(keys[5], 71), 0),
        "values": normal_values(keys[3], (ROWS, D), 1.0, 6.0, ((0, 32),)),
        "cotangent": normal_values(keys[4], (TOKENS, D), 1.0, 6.0, ((0, 256),)),
    }


def reference(slot_weight, slot_pos, touched, values, cotangent):
    blocks = TOKENS // TOK_DEV
    pos_b = slot_pos.reshape(blocks, TOK_DEV, TOPK)
    wgt_b = slot_weight.reshape(blocks, TOK_DEV, TOPK)
    cot_b = cotangent.reshape(blocks, TOK_DEV, D)

    def one_block(table, inputs):
        pos, wgt, cot, lists = inputs
        owner = (pos // CAP).astype(jnp.int32)
        within = (pos % CAP).astype(jnp.int32)
        rows = owner * ROWS_DEV + lists[owner, within]
        picked = values[rows].astype(jnp.float32)
        weights = wgt.astype(jnp.float32)
        grads = cot.astype(jnp.float32)
        bag = jnp.einsum("tk,tkd->td", weights, picked)
        wgrad = jnp.einsum("td,tkd->tk", grads, picked)
        terms = weights[:, :, None] * grads[:, None, :]
        table = table.at[rows.reshape(-1)].add(terms.reshape(-1, D))
        return table, (bag.astype(jnp.bfloat16), wgrad)

    start = jnp.zeros((ROWS, D), jnp.float32)
    table, (bags, wgrads) = lax.scan(one_block, start, (pos_b, wgt_b, cot_b, touched))
    return bags.reshape(TOKENS, D), wgrads.reshape(TOKENS, TOPK), table
```

```python
import jax
import jax.numpy as jnp
from jax import lax
from jax.experimental import pallas as pl
from jax.experimental.pallas import tpu as pltpu
from jax.sharding import Mesh
from jax.sharding import PartitionSpec as P

BF = jnp.bfloat16
F32 = jnp.float32
NZ, NX, ND = 8, 4, 8
NS = ND * NX
TOK = 128
CB = 128
CAP = 32
TOPK = 32
OWN = 256
GRP = NX * CAP
POS = NZ * GRP
R_W = TOK
R_C = R_W + TOPK
R_T = R_C + TOPK
R_ALL = R_T + 16
B_ALL = TOK + 2 * TOPK
VMEM = 56 * 1024 * 1024


def split(v):
    hi = v.astype(BF)
    return hi, (v - hi.astype(F32)).astype(BF)


def pack_kernel(z_ref, cot_ref, w_ref, pos_ref, list_ref, out_ref):
    z = z_ref[0]
    pos = pos_ref[...]
    plane = ((pos >> 7) - z) & (NZ - 1)
    code = ((pos & (GRP - 1)) + GRP) << plane
    code_t = code.astype(F32).T.astype(BF)
    w_t = w_ref[...].astype(F32).T.astype(BF)
    rows = [list_ref[pl.ds((z + h) & (NZ - 1), 1), :] for h in range(NZ)]
    lists = jnp.concatenate(rows + rows, axis=0).astype(F32).astype(BF)
    for i in range(out_ref.shape[0]):
        out_ref[i, 0:TOK, :] = cot_ref[:, i * CB:(i + 1) * CB]
        out_ref[i, R_W:R_C, :] = w_t
        out_ref[i, R_C:R_T, :] = code_t
        out_ref[i, R_T:R_ALL, :] = lists


def pack(z, cot, w, pos, lists):
    per = 8
    return pl.pallas_call(
        pack_kernel,
        grid=(NS // per,),
        in_specs=[
            pl.BlockSpec(memory_space=pltpu.SMEM),
            pl.BlockSpec((TOK, per * CB), lambda g: (0, g)),
            pl.BlockSpec((TOK, TOPK), lambda g: (0, 0)),
            pl.BlockSpec((TOK, TOPK), lambda g: (0, 0)),
            pl.BlockSpec((NZ, GRP), lambda g: (0, 0)),
        ],
        out_specs=pl.BlockSpec((per, R_ALL, CB), lambda g: (g, 0, 0)),
        out_shape=jax.ShapeDtypeStruct((NS, R_ALL, CB), BF),
        name="pack",
    )(z, cot, w, pos, lists)


def grads_kernel(z_ref, r_ref, wt_ref, out_ref, parts, lists):
    h = pl.program_id(0)

    @pl.when(h == 0)
    def _():
        for e in range(NS):
            lists[e * 16:(e + 1) * 16, :] = r_ref[e, R_T:R_ALL, :].astype(F32)

    sub = lax.broadcasted_iota(jnp.int32, (GRP, TOK), 0)
    codes = ((sub + GRP) << h).astype(F32).astype(BF)

    def one(e, carry):
        acc = jnp.zeros((GRP, TOK), BF)
        ce = r_ref[e, R_C:R_T, :]
        we = r_ref[e, R_W:R_C, :]
        for k in range(TOPK):
            acc = jnp.where(codes == ce[k:k + 1, :], we[k:k + 1, :], acc)
        wt_ref[e] = acc
        hi, lo = split(jnp.dot(acc, r_ref[e, 0:TOK, :], preferred_element_type=F32))
        for x in range(NX):
            parts[x, pl.ds(pl.multiple_of(e * CAP, CAP), CAP), 0:CB] = hi[x * CAP:(x + 1) * CAP]
            parts[x, pl.ds(pl.multiple_of(e * CAP, CAP), CAP), CB:2 * CB] = lo[x * CAP:(x + 1) * CAP]
        return carry

    lax.fori_loop(0, NS, one, 0)
    lane = lax.broadcasted_iota(jnp.int32, (8, GRP), 1) // CAP
    row = lax.broadcasted_iota(jnp.int32, (OWN, GRP), 0).astype(F32)
    raw = [lists[pl.ds(q * 16 + h, 8, stride=64), :] for q in range(4)]
    for x in range(NX):
        rows = jnp.zeros((8, GRP), F32)
        for q in range(4):
            rows = jnp.where(lane == q, pltpu.roll(raw[q], ((q - x) % 4) * CAP, 1), rows)
        total = jnp.zeros((OWN, 2 * CB), F32)
        for g in range(8):
            hot = jnp.where(row == rows[g:g + 1, :], 1.0, 0.0).astype(BF)
            total += jnp.dot(hot, parts[x, g * GRP:(g + 1) * GRP, :], preferred_element_type=F32)
        out_ref[0, x] = total[:, :CB] + total[:, CB:]


def grads(z, r):
    spec = pltpu.PrefetchScalarGridSpec(
        num_scalar_prefetch=1,
        grid=(NZ,),
        in_specs=[pl.BlockSpec((NS, R_ALL, CB), lambda h, z: (0, 0, 0))],
        out_specs=[
            pl.BlockSpec((NS, GRP, TOK), lambda h, z: (0, h, 0)),
            pl.BlockSpec((1, NX, OWN, CB), lambda h, z: ((z[0] + h) & (NZ - 1), 0, 0, 0)),
        ],
        scratch_shapes=[
            pltpu.VMEM((NX, NS * CAP, 2 * CB), BF),
            pltpu.VMEM((NS * 16, GRP), F32),
        ],
    )
    return pl.pallas_call(
        grads_kernel,
        grid_spec=spec,
        out_shape=[
            jax.ShapeDtypeStruct((NS, POS, TOK), BF),
            jax.ShapeDtypeStruct((NZ, NX, OWN, CB), F32),
        ],
        compiler_params=pltpu.CompilerParams(vmem_limit_bytes=VMEM),
        cost_estimate=pl.CostEstimate(flops=6 * 10**9, bytes_accessed=20 * 2**20, transcendentals=0),
        name="grads",
    )(z, r)


def bags_kernel(z_ref, r_ref, wt_ref, v_ref, out_ref, arrived, hots, lists):
    z = z_ref[0]
    for e in range(NS):
        lists[e * 16:(e + 1) * 16, :] = r_ref[e, R_T:R_ALL, :].astype(F32)
    col = lax.broadcasted_iota(jnp.int32, (GRP, OWN), 1).astype(F32)

    def fetch(h, carry):
        cols = lists[pl.ds(h, NS, stride=16), :].T
        for e in range(NS):
            hot = jnp.where(col == cols[:, e:e + 1], 1.0, 0.0).astype(BF)
            for x in range(NX):
                hots[x, e * CAP:(e + 1) * CAP, :] = hot[x * CAP:(x + 1) * CAP]
        for x in range(NX):
            got = jnp.dot(
                hots[x], v_ref[(z + h) & (NZ - 1), x], preferred_element_type=F32
            ).astype(BF)
            at = pl.multiple_of(h * GRP + x * CAP, CAP)
            for e in range(NS):
                arrived[e, pl.ds(at, CAP), :] = got[e * CAP:(e + 1) * CAP]
        return carry

    lax.fori_loop(0, NZ, fetch, 0)

    def one(e, carry):
        bag = lax.dot_general(
            wt_ref[e], arrived[e], (((0,), (0,)), ((), ())), preferred_element_type=F32
        )
        out_ref[e, 0:TOK, :] = bag.astype(BF)
        scores = lax.dot_general(
            r_ref[e, 0:TOK, :], arrived[e], (((1,), (1,)), ((), ())), preferred_element_type=F32
        )
        code = r_ref[e, R_C:R_T, :].astype(F32)
        code = jnp.concatenate([code] * (TOK // TOPK), axis=0).T.astype(jnp.int32)
        plane = jnp.zeros_like(code)
        for i in range(1, NZ):
            plane += (code >= (GRP << i)).astype(jnp.int32)
        within = (code >> plane) - GRP
        acc = jnp.zeros((TOK, GRP), F32)
        for h in range(NZ):
            tile = jnp.take_along_axis(
                scores[:, h * GRP:(h + 1) * GRP], within, axis=1, mode="promise_in_bounds"
            )
            acc = jnp.where(plane == h, tile, acc)
        hi, lo = split(acc.T[0:TOPK, :])
        out_ref[e, TOK:TOK + TOPK, :] = hi
        out_ref[e, TOK + TOPK:B_ALL, :] = lo
        return carry

    lax.fori_loop(0, NS, one, 0)


def bags(z, r, wt, v):
    vm = pl.BlockSpec(memory_space=pltpu.VMEM)
    return pl.pallas_call(
        bags_kernel,
        in_specs=[pl.BlockSpec(memory_space=pltpu.SMEM), vm, vm, vm],
        out_specs=vm,
        out_shape=jax.ShapeDtypeStruct((NS, B_ALL, CB), BF),
        scratch_shapes=[
            pltpu.VMEM((NS, POS, CB), BF),
            pltpu.VMEM((NX, NS * CAP, OWN), BF),
            pltpu.VMEM((NS * 16, GRP), F32),
        ],
        compiler_params=pltpu.CompilerParams(vmem_limit_bytes=VMEM),
        cost_estimate=pl.CostEstimate(flops=6 * 10**9, bytes_accessed=16 * 2**20, transcendentals=0),
        name="bags",
    )(z, r, wt, v)


def unpack_kernel(b_ref, out_ref, wg_ref, total):
    g = pl.program_id(0)
    part = jnp.zeros((TOPK, TOK), F32)
    for i in range(b_ref.shape[0]):
        out_ref[:, i * CB:(i + 1) * CB] = b_ref[i, 0:TOK, :]
        part += b_ref[i, TOK:TOK + TOPK, :].astype(F32) + b_ref[i, TOK + TOPK:B_ALL, :].astype(F32)
    part += jnp.where(g == 0, 0.0, total[...])
    total[...] = part
    wg_ref[...] = part.T


def unpack(b):
    per = 8
    return pl.pallas_call(
        unpack_kernel,
        grid=(NS // per,),
        in_specs=[pl.BlockSpec((per, B_ALL, CB), lambda g: (g, 0, 0))],
        out_specs=[
            pl.BlockSpec((TOK, per * CB), lambda g: (0, g)),
            pl.BlockSpec((TOK, TOPK), lambda g: (0, 0)),
        ],
        out_shape=[
            jax.ShapeDtypeStruct((TOK, NS * CB), BF),
            jax.ShapeDtypeStruct((TOK, TOPK), F32),
        ],
        scratch_shapes=[pltpu.VMEM((TOPK, TOK), F32)],
        name="unpack",
    )(b)


def on_device(slot_weight, slot_pos, touched, values, cotangent):
    z = lax.axis_index("z").astype(jnp.int32).reshape(1)
    d = lax.axis_index("dp")
    mine = lax.dynamic_slice(values, (0, d * (NX * CB)), (OWN, NX * CB))
    mine = mine.reshape(OWN, NX, CB).transpose(1, 0, 2)
    mine = lax.all_to_all(mine, "x", 0, 0, tiled=True)
    v = lax.all_gather(mine, "z")
    r = pack(z, cotangent, slot_weight, slot_pos, touched.reshape(NZ, GRP))
    r = lax.all_to_all(r, ("dp", "x"), 0, 0, tiled=True)
    wt, table = grads(z, r)
    table = lax.psum_scatter(table, "z", scatter_dimension=0, tiled=True)
    b = bags(z, r, wt, v)
    b = lax.all_to_all(b, ("dp", "x"), 0, 0, tiled=True)
    memory_out, weight_grad = unpack(b)
    table = lax.all_to_all(table.reshape(NX, OWN, CB), "x", 0, 0, tiled=True)
    value_grad = table.transpose(1, 0, 2).reshape(OWN, NX * CB)
    return memory_out, weight_grad, value_grad


def solution(mesh):
    cube = Mesh(mesh.devices.reshape(ND, NZ, NX), ("dp", "z", "x"))
    tokens = ("dp", "z", "x")
    return jax.shard_map(
        on_device,
        mesh=cube,
        in_specs=(
            P(tokens, None),
            P(tokens, None),
            P(tokens, None, None),
            P(("z", "x"), None),
            P(tokens, None),
        ),
        out_specs=(P(tokens, None), P(tokens, None), P(("z", "x"), "dp")),
        check_vma=False,
    )
```

```python
import jax
import jax.numpy as jnp
from jax import lax
from jax.experimental import pallas as pl
from jax.experimental.pallas import tpu as pltpu
from jax.sharding import Mesh
from jax.sharding import PartitionSpec as P

BF = jnp.bfloat16
F32 = jnp.float32
NZ, NX, ND = 8, 4, 8
NS = ND * NX
TOK = 128
CB = 128
CAP = 32
TOPK = 32
OWN = 256
GRP = NX * CAP
POS = NZ * GRP
M_C = TOPK
M_T = 2 * TOPK
M_ALL = M_T + 16
VMEM = 56 * 1024 * 1024


def split(v):
    hi = v.astype(BF)
    return hi, (v - hi.astype(F32)).astype(BF)


def slots_kernel(z_ref, w_ref, pos_ref, list_ref, out_ref):
    z = z_ref[0]
    pos = pos_ref[...]
    plane = ((pos >> 7) - z) & (NZ - 1)
    code = (((pos & (GRP - 1)) + GRP) << plane).astype(F32).astype(BF)
    rows = [list_ref[pl.ds((z + h) & (NZ - 1), 1), :] for h in range(NZ)]
    lists = jnp.concatenate(rows + rows, axis=0).astype(F32).astype(BF)
    w = w_ref[...]
    for i in range(NS):
        out_ref[i, 0:M_C, :] = w
        out_ref[i, M_C:M_T, :] = code
        out_ref[i, M_T:M_ALL, :] = lists


def cost(us):
    return pl.CostEstimate(flops=int(us * 1e9), bytes_accessed=2**20, transcendentals=0)


def slots(z, w, pos, lists):
    vm = pl.BlockSpec(memory_space=pltpu.VMEM)
    return pl.pallas_call(
        slots_kernel,
        in_specs=[pl.BlockSpec(memory_space=pltpu.SMEM), vm, vm, vm],
        out_specs=vm,
        out_shape=jax.ShapeDtypeStruct((NS, M_ALL, TOK), BF),
        cost_estimate=cost(2),
        name="slots",
    )(z, w, pos, lists)


def blocks_kernel(cot_ref, out_ref):
    for i in range(out_ref.shape[0]):
        out_ref[i] = cot_ref[:, i * CB:(i + 1) * CB]


def blocks(cot):
    per = 8
    return pl.pallas_call(
        blocks_kernel,
        grid=(NS // per,),
        in_specs=[pl.BlockSpec((TOK, per * CB), lambda g: (0, g))],
        out_specs=pl.BlockSpec((per, TOK, CB), lambda g: (g, 0, 0)),
        out_shape=jax.ShapeDtypeStruct((NS, TOK, CB), BF),
        cost_estimate=cost(2),
        name="blocks",
    )(cot)


def dense_kernel(m_ref, wt_ref):
    sub = lax.broadcasted_iota(jnp.int32, (GRP, TOK), 0)
    codes = ((sub + GRP) << pl.program_id(0)).astype(F32).astype(BF)

    def one(e, carry):
        acc = jnp.zeros((GRP, TOK), BF)
        we = m_ref[e, 0:M_C, :]
        ce = m_ref[e, M_C:M_T, :]
        for k in range(TOPK):
            acc = jnp.where(codes == ce[k:k + 1, :], we[k:k + 1, :], acc)
        wt_ref[e] = acc
        return carry

    lax.fori_loop(0, NS, one, 0, unroll=4)


def dense(m):
    return pl.pallas_call(
        dense_kernel,
        grid=(NZ,),
        in_specs=[pl.BlockSpec((NS, M_ALL, TOK), lambda h: (0, 0, 0))],
        out_specs=pl.BlockSpec((NS, GRP, TOK), lambda h: (0, h, 0)),
        out_shape=jax.ShapeDtypeStruct((NS, POS, TOK), BF),
        compiler_params=pltpu.CompilerParams(vmem_limit_bytes=VMEM),
        cost_estimate=cost(25),
        name="dense",
    )(m)


def grads_kernel(z_ref, m_ref, c_ref, wt_ref, out_ref, parts, lists):
    h = pl.program_id(0)

    @pl.when(h == 0)
    def _():
        for e in range(NS):
            lists[e * 16:(e + 1) * 16, :] = m_ref[e, M_T:M_ALL, :].astype(F32)

    for e in range(NS):
        hi, lo = split(jnp.dot(wt_ref[e], c_ref[e], preferred_element_type=F32))
        for x in range(NX):
            at = slice(e * CAP, (e + 1) * CAP)
            parts[x, at, 0:CB] = hi[x * CAP:(x + 1) * CAP]
            parts[x, at, CB:2 * CB] = lo[x * CAP:(x + 1) * CAP]
    lane = lax.broadcasted_iota(jnp.int32, (8, GRP), 1) // CAP
    row = lax.broadcasted_iota(jnp.int32, (OWN, GRP), 0).astype(F32).astype(BF)
    raw = [lists[pl.ds(q * 16 + h, 8, stride=64), :] for q in range(4)]
    for x in range(NX):
        rows = jnp.zeros((8, GRP), F32)
        for q in range(4):
            rows = jnp.where(lane == q, pltpu.roll(raw[q], ((q - x) % 4) * CAP, 1), rows)
        rows = rows.astype(BF)
        one, zero = jnp.ones((), BF), jnp.zeros((), BF)
        hot = jnp.concatenate([jnp.where(row == rows[g:g + 1, :], one, zero) for g in range(8)], axis=1)
        total = jnp.dot(hot, parts[x], preferred_element_type=F32)
        out_ref[0, x] = total[:, :CB] + total[:, CB:]


def grads(z, m, c, wt):
    whole = lambda h, z: (0, 0, 0)
    spec = pltpu.PrefetchScalarGridSpec(
        num_scalar_prefetch=1,
        grid=(NZ,),
        in_specs=[
            pl.BlockSpec((NS, M_ALL, TOK), whole),
            pl.BlockSpec((NS, TOK, CB), whole),
            pl.BlockSpec((NS, GRP, TOK), lambda h, z: (0, h, 0)),
        ],
        out_specs=pl.BlockSpec((1, NX, OWN, CB), lambda h, z: ((z[0] + h) & (NZ - 1), 0, 0, 0)),
        scratch_shapes=[
            pltpu.VMEM((NX, NS * CAP, 2 * CB), BF),
            pltpu.VMEM((NS * 16, GRP), F32),
        ],
    )
    return pl.pallas_call(
        grads_kernel,
        grid_spec=spec,
        out_shape=jax.ShapeDtypeStruct((NZ, NX, OWN, CB), F32),
        compiler_params=pltpu.CompilerParams(vmem_limit_bytes=VMEM),
        cost_estimate=cost(15),
        name="grads",
    )(z, m, c, wt)


EG = 8


def bags_kernel(z_ref, m_ref, wt_ref, v_ref, arrived_ref, out_ref, hots, lists):
    z = z_ref[0]
    for e in range(EG):
        lists[e * 16:(e + 1) * 16, :] = m_ref[e, M_T:M_ALL, :].astype(F32)
    col = lax.broadcasted_iota(jnp.int32, (GRP, OWN), 1).astype(F32)
    for h in range(NZ):
        cols = lists[pl.ds(h, EG, stride=16), :].T
        for e in range(EG):
            hot = jnp.where(col == cols[:, e:e + 1], 1.0, 0.0).astype(BF)
            for x in range(NX):
                hots[x, e * CAP:(e + 1) * CAP, :] = hot[x * CAP:(x + 1) * CAP]
        for x in range(NX):
            got = jnp.dot(
                hots[x], v_ref[(z + h) & (NZ - 1), x], preferred_element_type=F32
            ).astype(BF)
            at = h * GRP + x * CAP
            for e in range(EG):
                arrived_ref[e, at:at + CAP, :] = got[e * CAP:(e + 1) * CAP]
    for e in range(EG):
        bag = lax.dot_general(
            wt_ref[e], arrived_ref[e], (((0,), (0,)), ((), ())), preferred_element_type=F32
        )
        out_ref[e] = bag.astype(BF)


def bags(z, m, wt, v):
    part = lambda g: (g, 0, 0)
    return pl.pallas_call(
        bags_kernel,
        grid=(NS // EG,),
        in_specs=[
            pl.BlockSpec(memory_space=pltpu.SMEM),
            pl.BlockSpec((EG, M_ALL, TOK), part),
            pl.BlockSpec((EG, POS, TOK), part),
            pl.BlockSpec((NZ, NX, OWN, CB), lambda g: (0, 0, 0, 0)),
        ],
        out_specs=[pl.BlockSpec((EG, POS, CB), part), pl.BlockSpec((EG, TOK, CB), part)],
        out_shape=[
            jax.ShapeDtypeStruct((NS, POS, CB), BF),
            jax.ShapeDtypeStruct((NS, TOK, CB), BF),
        ],
        scratch_shapes=[
            pltpu.VMEM((NX, EG * CAP, OWN), BF),
            pltpu.VMEM((EG * 16, GRP), F32),
        ],
        compiler_params=pltpu.CompilerParams(vmem_limit_bytes=VMEM),
        cost_estimate=cost(18),
        name="bags",
    )(z, m, wt, v)


def scores_kernel(m_ref, c_ref, arrived_ref, out_ref):
    def one(e, carry):
        scores = lax.dot_general(
            c_ref[e], arrived_ref[e], (((1,), (1,)), ((), ())), preferred_element_type=F32
        )
        code = m_ref[e, M_C:M_T, :].astype(F32)
        code = jnp.concatenate([code] * (TOK // TOPK), axis=0).T.astype(jnp.int32)
        plane = jnp.zeros_like(code)
        for i in range(1, NZ):
            plane += (code >= (GRP << i)).astype(jnp.int32)
        within = (code >> plane) - GRP
        acc = jnp.zeros((TOK, GRP), F32)
        for h in range(NZ):
            tile = jnp.take_along_axis(
                scores[:, h * GRP:(h + 1) * GRP], within, axis=1, mode="promise_in_bounds"
            )
            acc = jnp.where(plane == h, tile, acc)
        out_ref[e] = acc.T[0:TOPK, :]
        return carry

    lax.fori_loop(0, EG, one, 0, unroll=2)


def scores(m, c, arrived):
    part = lambda g: (g, 0, 0)
    return pl.pallas_call(
        scores_kernel,
        grid=(NS // EG,),
        in_specs=[
            pl.BlockSpec((EG, M_ALL, TOK), part),
            pl.BlockSpec((EG, TOK, CB), part),
            pl.BlockSpec((EG, POS, CB), part),
        ],
        out_specs=pl.BlockSpec((EG, TOPK, TOK), part),
        out_shape=jax.ShapeDtypeStruct((NS, TOPK, TOK), F32),
        compiler_params=pltpu.CompilerParams(vmem_limit_bytes=VMEM),
        cost_estimate=cost(18),
        name="scores",
    )(m, c, arrived)


def gather_kernel(b_ref, out_ref):
    for i in range(b_ref.shape[0]):
        out_ref[:, i * CB:(i + 1) * CB] = b_ref[i]


def gather_blocks(b):
    per = 8
    rows = b.shape[1]
    return pl.pallas_call(
        gather_kernel,
        grid=(b.shape[0] // per,),
        in_specs=[pl.BlockSpec((per, rows, CB), lambda g: (g, 0, 0))],
        out_specs=pl.BlockSpec((rows, per * CB), lambda g: (0, g)),
        out_shape=jax.ShapeDtypeStruct((rows, b.shape[0] * CB), b.dtype),
        cost_estimate=cost(2),
        name="rows",
    )(b)


def on_device(slot_weight, slot_pos, touched, values, cotangent):
    z = lax.axis_index("z").astype(jnp.int32).reshape(1)
    d = lax.axis_index("dp")
    plane = ("dp", "x")
    m = slots(z, slot_weight.T, slot_pos.T, touched.reshape(NZ, GRP))
    m = lax.all_to_all(m, plane, 0, 0, tiled=True)
    mine = lax.dynamic_slice(values, (0, d * (NX * CB)), (OWN, NX * CB))
    mine = jnp.stack([mine[:, i * CB:(i + 1) * CB] for i in range(NX)])
    mine = lax.all_to_all(mine, "x", 0, 0, tiled=True)
    v = lax.all_gather(mine, "z")
    c = lax.all_to_all(blocks(cotangent), plane, 0, 0, tiled=True)
    wt = dense(m)
    table = grads(z, m, c, wt)
    arrived, b = bags(z, m, wt, v)
    b = lax.all_to_all(b, plane, 0, 0, tiled=True)
    b, g = lax.optimization_barrier((b, scores(m, c, arrived)))
    g = lax.all_to_all(g, plane, 0, 0, tiled=True)
    table = lax.psum_scatter(table, "z", scatter_dimension=0, tiled=True)
    table = lax.all_to_all(table.reshape(NX, OWN, CB), "x", 0, 0, tiled=True)
    value_grad = jnp.concatenate([table[i] for i in range(NX)], axis=1)
    return gather_blocks(b), g.sum(axis=0).T, value_grad


def solution(mesh):
    cube = Mesh(mesh.devices.reshape(ND, NZ, NX), ("dp", "z", "x"))
    tokens = ("dp", "z", "x")
    return jax.shard_map(
        on_device,
        mesh=cube,
        in_specs=(
            P(tokens, None),
            P(tokens, None),
            P(tokens, None, None),
            P(("z", "x"), None),
            P(tokens, None),
        ),
        out_specs=(P(tokens, None), P(tokens, None), P(("z", "x"), "dp")),
        check_vma=False,
    )
```

```python
import functools

import jax
import jax.numpy as jnp
from jax import lax
from jax.experimental import pallas as pl
from jax.experimental.pallas import tpu as pltpu
from jax.sharding import Mesh
from jax.sharding import PartitionSpec as P

BF = jnp.bfloat16
F32 = jnp.float32
NZ, NX, ND = 8, 4, 8
NS = ND * NX
TOK = 128
CB = 128
CAP = 32
TOPK = 32
OWN = 256
GRP = NX * CAP
POS = NZ * GRP
M_C = TOPK
M_T = 2 * TOPK
M_ALL = M_T + 16
VMEM = 48 * 1024 * 1024
SMALL = 16 * 1024 * 1024


def split(v):
    hi = v.astype(BF)
    return hi, (v - hi.astype(F32)).astype(BF)


def slots_kernel(z_ref, w_ref, pos_ref, list_ref, out_ref):
    z = z_ref[0]
    pos = pos_ref[...]
    plane = ((pos >> 7) - z) & (NZ - 1)
    code = (((pos & (GRP - 1)) + GRP) << plane).astype(F32).astype(BF)
    rows = [list_ref[pl.ds((z + h) & (NZ - 1), 1), :] for h in range(NZ)]
    lists = jnp.concatenate(rows + rows, axis=0).astype(F32).astype(BF)
    w = w_ref[...]
    for i in range(NS):
        out_ref[i, 0:M_C, :] = w
        out_ref[i, M_C:M_T, :] = code
        out_ref[i, M_T:M_ALL, :] = lists


def cost(us):
    return pl.CostEstimate(flops=int(us * 1e9), bytes_accessed=2**20, transcendentals=0)


def slots(z, w, pos, lists):
    vm = pl.BlockSpec(memory_space=pltpu.VMEM)
    return pl.pallas_call(
        slots_kernel,
        in_specs=[pl.BlockSpec(memory_space=pltpu.SMEM), vm, vm, vm],
        out_specs=vm,
        out_shape=jax.ShapeDtypeStruct((NS, M_ALL, TOK), BF),
        cost_estimate=cost(2),
        name="slots",
    )(z, w, pos, lists)


def blocks_kernel(cot_ref, out_ref):
    for i in range(out_ref.shape[0]):
        out_ref[i] = cot_ref[:, i * CB:(i + 1) * CB]


def blocks(cot):
    per = 8
    return pl.pallas_call(
        blocks_kernel,
        grid=(NS // per,),
        in_specs=[pl.BlockSpec((TOK, per * CB), lambda g: (0, g))],
        out_specs=pl.BlockSpec((per, TOK, CB), lambda g: (g, 0, 0)),
        out_shape=jax.ShapeDtypeStruct((NS, TOK, CB), BF),
        cost_estimate=cost(2),
        name="blocks",
    )(cot)


def dense_kernel(planes, m_ref, *wt_refs):
    sub = lax.broadcasted_iota(jnp.int32, (GRP, TOK), 0)
    for h, wt_ref in zip(planes, wt_refs):
        codes = ((sub + GRP) << h).astype(F32).astype(BF)

        def one(e, carry):
            acc = jnp.zeros((GRP, TOK), BF)
            we = m_ref[e, 0:M_C, :]
            ce = m_ref[e, M_C:M_T, :]
            for k in range(TOPK):
                acc = jnp.where(codes == ce[k:k + 1, :], we[k:k + 1, :], acc)
            wt_ref[e] = acc
            return carry

        lax.fori_loop(0, NS, one, 0, unroll=4)


def dense(m, planes):
    vm = pl.BlockSpec(memory_space=pltpu.VMEM)
    n = len(planes)
    return pl.pallas_call(
        functools.partial(dense_kernel, planes),
        in_specs=[vm],
        out_specs=[vm] * n,
        out_shape=[jax.ShapeDtypeStruct((NS, GRP, TOK), BF)] * n,
        compiler_params=pltpu.CompilerParams(vmem_limit_bytes=SMALL),
        cost_estimate=cost(3 * n),
        name="dense",
    )(m)


def grads_kernel(planes, m_ref, c_ref, *refs):
    n = len(planes)
    wt_refs, out_refs, (parts, lists) = refs[:n], refs[n:3 * n], refs[3 * n:]
    for e in range(NS):
        lists[e * 16:(e + 1) * 16, :] = m_ref[e, M_T:M_ALL, :].astype(F32)
    lane = lax.broadcasted_iota(jnp.int32, (8, GRP), 1) // CAP
    row = lax.broadcasted_iota(jnp.int32, (OWN, GRP), 0).astype(F32).astype(BF)
    one, zero = jnp.ones((), BF), jnp.zeros((), BF)
    for i, h in enumerate(planes):
        for e in range(NS):
            hi, lo = split(jnp.dot(wt_refs[i][e], c_ref[e], preferred_element_type=F32))
            for x in range(NX):
                at = slice(e * CAP, (e + 1) * CAP)
                parts[x, at, 0:CB] = hi[x * CAP:(x + 1) * CAP]
                parts[x, at, CB:2 * CB] = lo[x * CAP:(x + 1) * CAP]
        raw = [lists[pl.ds(q * 16 + h, 8, stride=64), :] for q in range(4)]
        for x in range(NX):
            rows = jnp.zeros((8, GRP), F32)
            for q in range(4):
                rows = jnp.where(lane == q, pltpu.roll(raw[q], ((q - x) % 4) * CAP, 1), rows)
            rows = rows.astype(BF)
            hot = jnp.concatenate(
                [jnp.where(row == rows[g:g + 1, :], one, zero) for g in range(8)], axis=1
            )
            total = jnp.dot(hot, parts[x], preferred_element_type=F32)
            out_refs[2 * i + x // 2][x % 2] = total[:, :CB] + total[:, CB:]


def grads(m, c, wts, planes):
    vm = pl.BlockSpec(memory_space=pltpu.VMEM)
    n = len(planes)
    outs = pl.pallas_call(
        functools.partial(grads_kernel, planes),
        in_specs=[vm] * (2 + n),
        out_specs=[vm] * (2 * n),
        out_shape=[jax.ShapeDtypeStruct((NX // 2, OWN, CB), F32)] * (2 * n),
        scratch_shapes=[
            pltpu.VMEM((NX, NS * CAP, 2 * CB), BF),
            pltpu.VMEM((NS * 16, GRP), F32),
        ],
        compiler_params=pltpu.CompilerParams(vmem_limit_bytes=SMALL),
        cost_estimate=cost(1 + 1.6 * n),
        name="grads",
    )(m, c, *wts)
    return [outs[2 * i:2 * i + 2] for i in range(n)]


EG = 8


def bags_kernel(later, x_ref, m_ref, *refs):
    wt_refs, v_refs, refs = refs[:NZ], refs[NZ:2 * NZ], refs[2 * NZ + later:]
    arrived_ref, out_ref, hots, lists = refs
    for e in range(EG):
        lists[e * 16:(e + 1) * 16, :] = m_ref[e, M_T:M_ALL, :].astype(F32)
    col = lax.broadcasted_iota(jnp.int32, (GRP, OWN), 1).astype(F32)
    for h in range(NZ):
        cols = lists[pl.ds(h, EG, stride=16), :].T
        for e in range(EG):
            hot = jnp.where(col == cols[:, e:e + 1], 1.0, 0.0).astype(BF)
            for x in range(NX):
                hots[x, e * CAP:(e + 1) * CAP, :] = hot[x * CAP:(x + 1) * CAP]
        for x in range(NX):
            got = jnp.dot(
                hots[x], v_refs[h][(x - x_ref[0]) & (NX - 1)], preferred_element_type=F32
            ).astype(BF)
            at = h * GRP + x * CAP
            for e in range(EG):
                arrived_ref[e, at:at + CAP, :] = got[e * CAP:(e + 1) * CAP]
    for e in range(EG):
        bag = lax.dot_general(
            jnp.concatenate([wt_ref[e] for wt_ref in wt_refs], axis=0), arrived_ref[e],
            (((0,), (0,)), ((), ())), preferred_element_type=F32,
        )
        out_ref[e] = bag.astype(BF)


STEPS = NS // EG // 2


def bags(x, m, wts, vs, earlier, half):
    part = lambda g: (g + half * STEPS, 0, 0)
    later = len(earlier)
    return pl.pallas_call(
        functools.partial(bags_kernel, later),
        grid=(STEPS,),
        in_specs=[
            pl.BlockSpec(memory_space=pltpu.SMEM),
            pl.BlockSpec((EG, M_ALL, TOK), part),
            *[pl.BlockSpec((EG, GRP, TOK), part)] * NZ,
            *[pl.BlockSpec((NX, OWN, CB), lambda g: (0, 0, 0))] * NZ,
            *[pl.BlockSpec(memory_space=pl.ANY)] * later,
        ],
        out_specs=[pl.BlockSpec((EG, POS, CB), lambda g: (g, 0, 0)), pl.BlockSpec((EG, TOK, CB), part)],
        out_shape=[
            jax.ShapeDtypeStruct((EG * STEPS, POS, CB), BF),
            jax.ShapeDtypeStruct((NS, TOK, CB), BF),
        ],
        scratch_shapes=[
            pltpu.VMEM((NX, EG * CAP, OWN), BF),
            pltpu.VMEM((EG * 16, GRP), F32),
        ],
        input_output_aliases={2 + 2 * NZ: 1} if later else {},
        compiler_params=pltpu.CompilerParams(vmem_limit_bytes=VMEM),
        cost_estimate=cost(8),
        name="bags",
    )(x, m, *wts, *vs, *earlier)


def scores_kernel(m_ref, c_ref, arrived_ref, *refs):
    out_ref = refs[-1]

    def one(e, carry):
        scores = lax.dot_general(
            c_ref[e], arrived_ref[e], (((1,), (1,)), ((), ())), preferred_element_type=F32
        )
        code = m_ref[e, M_C:M_T, :].astype(F32)
        code = jnp.concatenate([code] * (TOK // TOPK), axis=0).T.astype(jnp.int32)
        plane = jnp.zeros_like(code)
        for i in range(1, NZ):
            plane += (code >= (GRP << i)).astype(jnp.int32)
        within = (code >> plane) - GRP
        acc = jnp.zeros((TOK, GRP), F32)
        for h in range(NZ):
            tile = jnp.take_along_axis(
                scores[:, h * GRP:(h + 1) * GRP], within, axis=1, mode="promise_in_bounds"
            )
            acc = jnp.where(plane == h, tile, acc)
        out_ref[e] = acc.T[0:TOPK, :]
        return carry

    lax.fori_loop(0, EG, one, 0, unroll=2)


def scores(m, c, arrived, earlier, half):
    part = lambda g: (g + half * STEPS, 0, 0)
    later = len(earlier)
    return pl.pallas_call(
        scores_kernel,
        grid=(STEPS,),
        in_specs=[
            pl.BlockSpec((EG, M_ALL, TOK), part),
            pl.BlockSpec((EG, TOK, CB), part),
            pl.BlockSpec((EG, POS, CB), lambda g: (g, 0, 0)),
            *[pl.BlockSpec(memory_space=pl.ANY)] * later,
        ],
        out_specs=pl.BlockSpec((EG, TOPK, TOK), part),
        out_shape=jax.ShapeDtypeStruct((NS, TOPK, TOK), F32),
        input_output_aliases={3: 0} if later else {},
        compiler_params=pltpu.CompilerParams(vmem_limit_bytes=VMEM),
        cost_estimate=cost(9),
        name="scores",
    )(m, c, arrived, *earlier)


def gather_kernel(b_ref, out_ref):
    for i in range(b_ref.shape[0]):
        out_ref[:, i * CB:(i + 1) * CB] = b_ref[i]


def gather_blocks(b):
    per = 8
    rows = b.shape[1]
    return pl.pallas_call(
        gather_kernel,
        grid=(b.shape[0] // per,),
        in_specs=[pl.BlockSpec((per, rows, CB), lambda g: (g, 0, 0))],
        out_specs=pl.BlockSpec((rows, per * CB), lambda g: (0, g)),
        out_shape=jax.ShapeDtypeStruct((rows, b.shape[0] * CB), b.dtype),
        cost_estimate=cost(2),
        name="rows",
    )(b)


UP = [(i, (i + 1) % NZ) for i in range(NZ)]
DOWN = [(i, (i - 1) % NZ) for i in range(NZ)]


def up(v):
    return lax.ppermute(v, "z", UP)


def down(v):
    return lax.ppermute(v, "z", DOWN)


def columns_kernel(x_ref, *refs):
    out_ref = refs[NX]
    for i in range(NX):
        at = pl.multiple_of(((x_ref[0] - i) & (NX - 1)) * CB, CB)
        out_ref[:, pl.ds(at, CB)] = refs[i][...]


def columns(x, cols):
    vm = pl.BlockSpec(memory_space=pltpu.VMEM)
    return pl.pallas_call(
        columns_kernel,
        in_specs=[pl.BlockSpec(memory_space=pltpu.SMEM)] + [vm] * NX,
        out_specs=vm,
        out_shape=jax.ShapeDtypeStruct((OWN, NX * CB), F32),
        cost_estimate=cost(1),
        name="columns",
    )(x, *cols)


def after(first, then):
    return lax.optimization_barrier((first, then))[1]


def on_device(slot_weight, slot_pos, touched, values, cotangent):
    z = lax.axis_index("z").astype(jnp.int32).reshape(1)
    d = lax.axis_index("dp").astype(jnp.int32)
    x = lax.axis_index("x").astype(jnp.int32)
    plane = ("dp", "x")
    m = slots(z, slot_weight.T, slot_pos.T, touched.reshape(NZ, GRP))
    m, cotangent = lax.optimization_barrier((m, cotangent))
    m = lax.all_to_all(m, plane, 0, 0, tiled=True)
    c, values = lax.optimization_barrier((blocks(cotangent), values))
    mine = []
    for i in range(NX):
        to = (x - i) & (NX - 1)
        part = lax.dynamic_slice(values, (0, (d * NX + to) * CB), (OWN, CB))
        mine.append(lax.ppermute(part, "x", [(j, (j - i) % NX) for j in range(NX)]) if i else part)
    mine = jnp.stack(mine)
    c = lax.all_to_all(c, plane, 0, 0, tiled=True)
    wt, p = [None] * NZ, [None] * NZ

    def weigh(*planes):
        for h, w in zip(planes, dense(m, planes)):
            wt[h] = w

    def grade(*planes):
        for h, q in zip(planes, grads(m, c, [wt[h] for h in planes], planes)):
            p[h] = q

    v = [mine] + [None] * (NZ - 1)
    v[7], v[1] = up(v[0]), down(v[0])
    weigh(4)
    v[7], v[1] = after(wt[4], (v[7], v[1]))
    v[6], v[2] = up(v[7]), down(v[1])
    weigh(3, 5)
    weigh(2, 6)
    v[6], v[2] = after(wt[2], (v[6], v[2]))
    v[5], v[3] = up(v[6]), down(v[2])
    weigh(1, 7)
    weigh(0)
    v[5], v[3] = after(wt[1], (v[5], v[3]))
    v[4] = jnp.concatenate([up(v[5][:NX // 2]), down(v[3][NX // 2:])])
    grade(4)
    a_up, b_down = up(p[4][0]), down(p[4][1])
    grade(3, 5)
    b_up, a_down = up(p[3][1]), down(p[5][0])
    grade(2, 6)
    a_up, b_down = after(p[2][0], p[3][0] + a_up), after(p[6][1], p[5][1] + b_down)
    wt[1], _ = lax.optimization_barrier((wt[1], (a_up, b_down)))
    a_up, b_down = up(a_up), down(b_down)
    grade(1, 7)
    wt[0], _ = lax.optimization_barrier((wt[0], p[1][0]))
    grade(0)
    wt[4], _ = lax.optimization_barrier((wt[4], p[0][0]))
    got0, b = bags(x.reshape(1), m, wt, v, [], 0)
    sums = [p[2][0] + a_up, p[2][1] + b_up, p[6][0] + a_down, p[6][1] + b_down]
    b, sums = lax.optimization_barrier((b, sums))
    a_up, b_up, a_down, b_down = up(sums[0]), up(sums[1]), down(sums[2]), down(sums[3])
    got1, b = bags(x.reshape(1), m, wt, v, [b], 1)
    b, got0 = lax.optimization_barrier((b, got0))
    b = lax.all_to_all(b, plane, 0, 0, tiled=True)
    g = scores(m, c, got0, [], 0)
    sums = [p[1][0] + a_up, p[1][1] + b_up, p[7][0] + a_down, p[7][1] + b_down]
    g, sums = lax.optimization_barrier((g, sums))
    a_up, b_up, a_down, b_down = up(sums[0]), up(sums[1]), down(sums[2]), down(sums[3])
    g = scores(m, c, got1, [g], 1)
    sums = [a_up, b_up, a_down, b_down]
    b, g, sums = lax.optimization_barrier((b, g, sums))
    a_up, b_up, a_down, b_down = sums
    g = lax.all_to_all(g, plane, 0, 0, tiled=True)
    table = jnp.concatenate([p[0][0] + a_up + a_down, p[0][1] + b_up + b_down])
    cols = []
    for i in range(NX):
        part = lax.dynamic_index_in_dim(table, (x + i) & (NX - 1), 0, False)
        cols.append(lax.ppermute(part, "x", [(j, (j + i) % NX) for j in range(NX)]) if i else part)
    value_grad = columns(x.reshape(1), cols)
    return gather_blocks(b), g.sum(axis=0).T, value_grad


def solution(mesh):
    cube = Mesh(mesh.devices.reshape(ND, NZ, NX), ("dp", "z", "x"))
    tokens = ("dp", "z", "x")
    return jax.shard_map(
        on_device,
        mesh=cube,
        in_specs=(
            P(tokens, None),
            P(tokens, None),
            P(tokens, None, None),
            P(("z", "x"), None),
            P(tokens, None),
        ),
        out_specs=(P(tokens, None), P(tokens, None), P(("z", "x"), "dp")),
        check_vma=False,
    )
```

```python
import jax
import jax.numpy as jnp
from jax import lax
from jax.experimental import pallas as pl
from jax.experimental.pallas import tpu as pltpu
from jax.sharding import Mesh
from jax.sharding import PartitionSpec as P

BF = jnp.bfloat16
F32 = jnp.float32
NZ, NX, ND = 8, 4, 8
NS = ND * NX
TOK = 128
CB = 128
CAP = 32
TOPK = 32
OWN = 256
GRP = NX * CAP
POS = NZ * GRP
M_C = TOPK
M_T = 2 * TOPK
M_V = M_T + 16
PIECE = OWN // ND
M_ALL = M_V + PIECE
VMEM = 56 * 1024 * 1024


def split(v):
    hi = v.astype(BF)
    return hi, (v - hi.astype(F32)).astype(BF)


def slots_kernel(at_ref, w_ref, pos_ref, list_ref, v_ref, out_ref, wide):
    z = at_ref[0]
    pos = pos_ref[...]
    plane = ((pos >> 7) - z) & (NZ - 1)
    code = (((pos & (GRP - 1)) + GRP) << plane).astype(F32).astype(BF)
    lists = list_ref[0]
    owner = lax.broadcasted_iota(jnp.int32, (NX * NZ, GRP), 0) & (NX - 1)
    lane = lax.broadcasted_iota(jnp.int32, (NX * NZ, GRP), 1) // CAP
    wide[...] = jnp.where(owner == lane, jnp.concatenate([lists] * NX, axis=1), 0)
    rows = []
    for h in range(NZ):
        four = [wide[pl.ds(((z + h) & (NZ - 1)) * NX + i, 1), :] for i in range(NX)]
        rows.append(four[0] + four[1] + four[2] + four[3])
    lists = jnp.concatenate(rows + rows, axis=0).astype(F32).astype(BF)
    w = w_ref[...]
    for i in range(NS):
        out_ref[i, 0:M_C, :] = w
        out_ref[i, M_C:M_T, :] = code
        out_ref[i, M_T:M_V, :] = lists
        out_ref[i, M_V:M_ALL, :] = v_ref[:, i * CB:(i + 1) * CB]


def cost(us):
    return pl.CostEstimate(flops=int(us * 1e9), bytes_accessed=2**20, transcendentals=0)


def slots(at, w, pos, lists, values):
    spec = pltpu.PrefetchScalarGridSpec(
        num_scalar_prefetch=1,
        grid=(1,),
        in_specs=[
            pl.BlockSpec((TOPK, TOK), lambda i, at: (0, 0)),
            pl.BlockSpec((TOPK, TOK), lambda i, at: (0, 0)),
            pl.BlockSpec((1, NX * NZ, CAP), lambda i, at: (0, 0, 0)),
            pl.BlockSpec((PIECE, NS * CB), lambda i, at: (at[1], 0)),
        ],
        out_specs=pl.BlockSpec((NS, M_ALL, TOK), lambda i, at: (0, 0, 0)),
        scratch_shapes=[pltpu.VMEM((NX * NZ, GRP), jnp.int32)],
    )
    return pl.pallas_call(
        slots_kernel,
        grid_spec=spec,
        out_shape=jax.ShapeDtypeStruct((NS, M_ALL, TOK), BF),
        compiler_params=pltpu.CompilerParams(vmem_limit_bytes=VMEM),
        cost_estimate=cost(2),
        name="slots",
    )(at, w, pos, lists, values)


def blocks_kernel(cot_ref, out_ref):
    for i in range(out_ref.shape[0]):
        out_ref[i] = cot_ref[:, i * CB:(i + 1) * CB]


def blocks(cot):
    per = 8
    return pl.pallas_call(
        blocks_kernel,
        grid=(NS // per,),
        in_specs=[pl.BlockSpec((TOK, per * CB), lambda g: (0, g))],
        out_specs=pl.BlockSpec((per, TOK, CB), lambda g: (g, 0, 0)),
        out_shape=jax.ShapeDtypeStruct((NS, TOK, CB), BF),
        cost_estimate=cost(2),
        name="blocks",
    )(cot)


def dense_kernel(m_ref, wt_ref):
    sub = lax.broadcasted_iota(jnp.int32, (GRP, TOK), 0)
    codes = ((sub + GRP) << pl.program_id(0)).astype(F32).astype(BF)

    def one(e, carry):
        acc = jnp.zeros((GRP, TOK), BF)
        we = m_ref[e, 0:M_C, :]
        ce = m_ref[e, M_C:M_T, :]
        for k in range(TOPK):
            acc = jnp.where(codes == ce[k:k + 1, :], we[k:k + 1, :], acc)
        wt_ref[e] = acc
        return carry

    lax.fori_loop(0, NS, one, 0, unroll=4)


def dense(m):
    return pl.pallas_call(
        dense_kernel,
        grid=(NZ,),
        in_specs=[pl.BlockSpec((NS, M_T, TOK), lambda h: (0, 0, 0))],
        out_specs=pl.BlockSpec((NS, GRP, TOK), lambda h: (0, h, 0)),
        out_shape=jax.ShapeDtypeStruct((NS, POS, TOK), BF),
        compiler_params=pltpu.CompilerParams(vmem_limit_bytes=VMEM),
        cost_estimate=cost(25),
        name="dense",
    )(m)


def grads_kernel(at_ref, t_ref, c_ref, wt0_ref, wt1_ref, out_ref, parts, lists):
    q = pl.program_id(0)

    @pl.when(q == 0)
    def _():
        for e in range(NS):
            lists[e * 16:(e + 1) * 16, :] = t_ref[e].astype(F32)

    lane = lax.broadcasted_iota(jnp.int32, (8, GRP), 1) // CAP
    row = lax.broadcasted_iota(jnp.int32, (OWN, GRP), 0).astype(F32).astype(BF)
    one, zero = jnp.ones((), BF), jnp.zeros((), BF)
    for i, wt_ref in enumerate((wt0_ref, wt1_ref)):
        h = (2 * q + i - at_ref[0]) & (NZ - 1)
        for e in range(NS):
            hi, lo = split(jnp.dot(wt_ref[e], c_ref[e], preferred_element_type=F32))
            for x in range(NX):
                at = slice(e * CAP, (e + 1) * CAP)
                parts[i, x, at, 0:CB] = hi[x * CAP:(x + 1) * CAP]
                parts[i, x, at, CB:2 * CB] = lo[x * CAP:(x + 1) * CAP]
        raw = [lists[pl.ds(j * 16 + h, 8, stride=64), :] for j in range(4)]
        for x in range(NX):
            rows = jnp.zeros((8, GRP), F32)
            for j in range(4):
                rows = jnp.where(lane == j, pltpu.roll(raw[j], ((j - x) % 4) * CAP, 1), rows)
            rows = rows.astype(BF)
            hot = jnp.concatenate(
                [jnp.where(row == rows[g:g + 1, :], one, zero) for g in range(8)], axis=1
            )
            total = jnp.dot(hot, parts[i, x], preferred_element_type=F32)
            out_ref[i, x] = total[:, :CB] + total[:, CB:]


def grads(at, m, c, wt):
    spec = pltpu.PrefetchScalarGridSpec(
        num_scalar_prefetch=1,
        grid=(NZ // 2,),
        in_specs=[
            pl.BlockSpec((NS, 16, TOK), lambda q, at: (0, M_T // 16, 0)),
            pl.BlockSpec((NS, TOK, CB), lambda q, at: (0, 0, 0)),
            pl.BlockSpec((NS, GRP, TOK), lambda q, at: (0, (2 * q - at[0]) & (NZ - 1), 0)),
            pl.BlockSpec((NS, GRP, TOK), lambda q, at: (0, (2 * q + 1 - at[0]) & (NZ - 1), 0)),
        ],
        out_specs=pl.BlockSpec((2, NX, OWN, CB), lambda q, at: (q, 0, 0, 0)),
        scratch_shapes=[
            pltpu.VMEM((2, NX, NS * CAP, 2 * CB), BF),
            pltpu.VMEM((NS * 16, GRP), F32),
        ],
    )
    return pl.pallas_call(
        grads_kernel,
        grid_spec=spec,
        out_shape=jax.ShapeDtypeStruct((NZ, NX, OWN, CB), F32),
        compiler_params=pltpu.CompilerParams(vmem_limit_bytes=VMEM),
        cost_estimate=cost(12),
        name="grads",
    )(at, m, c, wt, wt)


EG = 8


def bags_kernel(at_ref, t_ref, wt_ref, v_ref, arrived_ref, out_ref, hots, lists):
    z = at_ref[0]
    for e in range(EG):
        lists[e * 16:(e + 1) * 16, :] = t_ref[e].astype(F32)
    col = lax.broadcasted_iota(jnp.int32, (GRP, OWN), 1).astype(F32)
    for h in range(NZ):
        cols = lists[pl.ds(h, EG, stride=16), :].T
        for e in range(EG):
            hot = jnp.where(col == cols[:, e:e + 1], 1.0, 0.0).astype(BF)
            for x in range(NX):
                hots[x, e * CAP:(e + 1) * CAP, :] = hot[x * CAP:(x + 1) * CAP]
        for x in range(NX):
            rows = jnp.concatenate(
                [v_ref[(z + h) & (NZ - 1), d * NX + x] for d in range(ND)], axis=0
            )
            got = jnp.dot(hots[x], rows, preferred_element_type=F32).astype(BF)
            at = h * GRP + x * CAP
            for e in range(EG):
                arrived_ref[e, at:at + CAP, :] = got[e * CAP:(e + 1) * CAP]
    for e in range(EG):
        bag = lax.dot_general(
            wt_ref[e], arrived_ref[e], (((0,), (0,)), ((), ())), preferred_element_type=F32
        )
        out_ref[e] = bag.astype(BF)


def bags(at, m, wt, v):
    part = lambda g: (g, 0, 0)
    return pl.pallas_call(
        bags_kernel,
        grid=(NS // EG,),
        in_specs=[
            pl.BlockSpec(memory_space=pltpu.SMEM),
            pl.BlockSpec((EG, 16, TOK), lambda g: (g, M_T // 16, 0)),
            pl.BlockSpec((EG, POS, TOK), part),
            pl.BlockSpec((NZ, NS, PIECE, CB), lambda g: (0, 0, 0, 0)),
        ],
        out_specs=[pl.BlockSpec((EG, POS, CB), part), pl.BlockSpec((EG, TOK, CB), part)],
        out_shape=[
            jax.ShapeDtypeStruct((NS, POS, CB), BF),
            jax.ShapeDtypeStruct((NS, TOK, CB), BF),
        ],
        scratch_shapes=[
            pltpu.VMEM((NX, EG * CAP, OWN), BF),
            pltpu.VMEM((EG * 16, GRP), F32),
        ],
        compiler_params=pltpu.CompilerParams(vmem_limit_bytes=VMEM),
        cost_estimate=cost(18),
        name="bags",
    )(at, m, wt, v)


def scores_kernel(m_ref, c_ref, arrived_ref, out_ref):
    def one(e, carry):
        scores = lax.dot_general(
            c_ref[e], arrived_ref[e], (((1,), (1,)), ((), ())), preferred_element_type=F32
        )
        code = m_ref[e].astype(F32)
        code = jnp.concatenate([code] * (TOK // TOPK), axis=0).T.astype(jnp.int32)
        plane = jnp.zeros_like(code)
        for i in range(1, NZ):
            plane += (code >= (GRP << i)).astype(jnp.int32)
        within = (code >> plane) - GRP
        acc = jnp.zeros((TOK, GRP), F32)
        for h in range(NZ):
            tile = jnp.take_along_axis(
                scores[:, h * GRP:(h + 1) * GRP], within, axis=1, mode="promise_in_bounds"
            )
            acc = jnp.where(plane == h, tile, acc)
        out_ref[e] = acc.T[0:TOPK, :]
        return carry

    lax.fori_loop(0, EG, one, 0, unroll=2)


def scores(m, c, arrived):
    part = lambda g: (g, 0, 0)
    return pl.pallas_call(
        scores_kernel,
        grid=(NS // EG,),
        in_specs=[
            pl.BlockSpec((EG, TOPK, TOK), lambda g: (g, 1, 0)),
            pl.BlockSpec((EG, TOK, CB), part),
            pl.BlockSpec((EG, POS, CB), part),
        ],
        out_specs=pl.BlockSpec((EG, TOPK, TOK), part),
        out_shape=jax.ShapeDtypeStruct((NS, TOPK, TOK), F32),
        compiler_params=pltpu.CompilerParams(vmem_limit_bytes=VMEM),
        cost_estimate=cost(18),
        name="scores",
    )(m, c, arrived)


def gather_kernel(b_ref, out_ref):
    for i in range(b_ref.shape[0]):
        out_ref[:, i * CB:(i + 1) * CB] = b_ref[i]


def gather_blocks(b):
    per = 8
    rows = b.shape[1]
    return pl.pallas_call(
        gather_kernel,
        grid=(b.shape[0] // per,),
        in_specs=[pl.BlockSpec((per, rows, CB), lambda g: (g, 0, 0))],
        out_specs=pl.BlockSpec((rows, per * CB), lambda g: (0, g)),
        out_shape=jax.ShapeDtypeStruct((rows, b.shape[0] * CB), b.dtype),
        cost_estimate=cost(2),
        name="rows",
    )(b)


def on_device(slot_weight, slot_pos, touched, values, cotangent):
    at = jnp.stack([lax.axis_index("z"), lax.axis_index("dp")]).astype(jnp.int32)
    plane = ("dp", "x")
    m = slots(at, slot_weight.T, slot_pos.T, touched, values)
    m = lax.all_to_all(m, plane, 0, 0, tiled=True)
    m, c = lax.optimization_barrier((m, blocks(cotangent)))
    v = lax.all_gather(m[:, M_V:, :], "z")
    c = lax.all_to_all(c, plane, 0, 0, tiled=True)
    wt = dense(m)
    table = grads(at, m, c, wt)
    arrived, b = bags(at, m, wt, v)
    b = lax.all_to_all(b, plane, 0, 0, tiled=True)
    b, g = lax.optimization_barrier((b, scores(m, c, arrived)))
    g = lax.all_to_all(g, plane, 0, 0, tiled=True)
    table = lax.psum_scatter(table, "z", scatter_dimension=0, tiled=True)
    table = lax.all_to_all(table.reshape(NX, OWN, CB), "x", 0, 0, tiled=True)
    value_grad = jnp.concatenate([table[i] for i in range(NX)], axis=1)
    return gather_blocks(b), g.sum(axis=0).T, value_grad


def solution(mesh):
    cube = Mesh(mesh.devices.reshape(ND, NZ, NX), ("dp", "z", "x"))
    tokens = ("dp", "z", "x")
    return jax.shard_map(
        on_device,
        mesh=cube,
        in_specs=(
            P(tokens, None),
            P(tokens, None),
            P(tokens, None, None),
            P(("z", "x"), None),
            P(tokens, None),
        ),
        out_specs=(P(tokens, None), P(tokens, None), P(("z", "x"), "dp")),
        check_vma=False,
    )
```

```python
import jax
import jax.numpy as jnp
from jax import lax
from jax.experimental import pallas as pl
from jax.experimental.pallas import tpu as pltpu
from jax.sharding import Mesh
from jax.sharding import PartitionSpec as P

BF = jnp.bfloat16
F32 = jnp.float32
NZ, NX, ND = 8, 4, 8
NS = ND * NX
TOK = 128
CB = 128
CAP = 32
TOPK = 32
OWN = 256
GRP = NX * CAP
POS = NZ * GRP
M_C = TOPK
M_T = 2 * TOPK
M_ALL = M_T + 16
MIB = 1024 * 1024


def split(v):
    hi = v.astype(BF)
    return hi, (v - hi.astype(F32)).astype(BF)


def slots_kernel(at_ref, w_ref, pos_ref, list_ref, out_ref, wide):
    z = at_ref[0]
    pos = pos_ref[...]
    plane = ((pos >> 7) - z) & (NZ - 1)
    code = (((pos & (GRP - 1)) + GRP) << plane).astype(F32).astype(BF)
    lists = list_ref[0]
    owner = lax.broadcasted_iota(jnp.int32, (NX * NZ, GRP), 0) & (NX - 1)
    lane = lax.broadcasted_iota(jnp.int32, (NX * NZ, GRP), 1) // CAP
    wide[...] = jnp.where(owner == lane, jnp.concatenate([lists] * NX, axis=1), 0)
    rows = []
    for h in range(NZ):
        four = [wide[pl.ds(((z + h) & (NZ - 1)) * NX + i, 1), :] for i in range(NX)]
        rows.append(four[0] + four[1] + four[2] + four[3])
    lists = jnp.concatenate(rows + rows, axis=0).astype(F32).astype(BF)
    w = w_ref[...]
    for i in range(NS):
        out_ref[i, 0:M_C, :] = w
        out_ref[i, M_C:M_T, :] = code
        out_ref[i, M_T:M_ALL, :] = lists


def cost(us):
    return pl.CostEstimate(flops=int(us * 1e9), bytes_accessed=2**20, transcendentals=0)


def slots(at, w, pos, lists):
    spec = pltpu.PrefetchScalarGridSpec(
        num_scalar_prefetch=1,
        grid=(1,),
        in_specs=[
            pl.BlockSpec((TOPK, TOK), lambda i, at: (0, 0)),
            pl.BlockSpec((TOPK, TOK), lambda i, at: (0, 0)),
            pl.BlockSpec((1, NX * NZ, CAP), lambda i, at: (0, 0, 0)),
        ],
        out_specs=pl.BlockSpec((NS, M_ALL, TOK), lambda i, at: (0, 0, 0)),
        scratch_shapes=[pltpu.VMEM((NX * NZ, GRP), jnp.int32)],
    )
    return pl.pallas_call(
        slots_kernel,
        grid_spec=spec,
        out_shape=jax.ShapeDtypeStruct((NS, M_ALL, TOK), BF),
        compiler_params=pltpu.CompilerParams(vmem_limit_bytes=56 * MIB),
        cost_estimate=cost(2),
        name="slots",
    )(at, w, pos, lists)


def blocks_kernel(cot_ref, out_ref):
    for i in range(out_ref.shape[0]):
        out_ref[i] = cot_ref[:, i * CB:(i + 1) * CB]


def blocks(cot):
    per = 8
    return pl.pallas_call(
        blocks_kernel,
        grid=(NS // per,),
        in_specs=[pl.BlockSpec((TOK, per * CB), lambda g: (0, g))],
        out_specs=pl.BlockSpec((per, TOK, CB), lambda g: (g, 0, 0)),
        out_shape=jax.ShapeDtypeStruct((NS, TOK, CB), BF),
        cost_estimate=cost(2),
        name="blocks",
    )(cot)


def dense_kernel(m_ref, wt_ref):
    sub = lax.broadcasted_iota(jnp.int32, (GRP, TOK), 0)
    codes = ((sub + GRP) << (2 * pl.program_id(0))).astype(F32).astype(BF)
    tile = 16
    tiles = [codes[i:i + tile] for i in range(0, GRP, tile)]

    def one(e, carry):
        accs = [[jnp.zeros((tile, TOK), BF) for _ in tiles] for _ in range(2)]
        we = m_ref[e, 0:M_C, :]
        ce = m_ref[e, M_C:M_T, :]
        for k in range(TOPK):
            w = jnp.broadcast_to(we[k:k + 1, :], (tile, TOK))
            at = jnp.broadcast_to(ce[k:k + 1, :], (tile, TOK))
            for acc in accs:
                for i, t in enumerate(tiles):
                    acc[i] = jnp.where(t == at, w, acc[i])
                at = at * jnp.asarray(0.5, BF)
        for j, acc in enumerate(accs):
            for i, t in enumerate(acc):
                wt_ref[e, j * GRP + i * tile:j * GRP + (i + 1) * tile, :] = t
        return carry

    lax.fori_loop(0, NS, one, 0, unroll=4)


def dense(m):
    return pl.pallas_call(
        dense_kernel,
        grid=(NZ // 2,),
        in_specs=[pl.BlockSpec((NS, M_T, TOK), lambda h: (0, 0, 0))],
        out_specs=pl.BlockSpec((NS, 2 * GRP, TOK), lambda h: (0, h, 0)),
        out_shape=jax.ShapeDtypeStruct((NS, POS, TOK), BF),
        compiler_params=pltpu.CompilerParams(vmem_limit_bytes=56 * MIB),
        cost_estimate=cost(25),
        name="dense",
    )(m)


def grads_kernel(at_ref, t_ref, c_ref, wt0_ref, wt1_ref, out_ref, parts, lists):
    q = pl.program_id(0)

    @pl.when(q == 0)
    def _():
        for e in range(NS):
            lists[e * 16:(e + 1) * 16, :] = t_ref[e].astype(F32)

    lane = lax.broadcasted_iota(jnp.int32, (8, GRP), 1) // CAP
    row = lax.broadcasted_iota(jnp.int32, (OWN, GRP), 0).astype(F32).astype(BF)
    one, zero = jnp.ones((), BF), jnp.zeros((), BF)
    for i, wt_ref in enumerate((wt0_ref, wt1_ref)):
        h = (2 * q + i - at_ref[0]) & (NZ - 1)
        for e in range(NS):
            hi, lo = split(jnp.dot(wt_ref[e], c_ref[e], preferred_element_type=F32))
            for x in range(NX):
                at = slice(e * CAP, (e + 1) * CAP)
                parts[i, x, at, 0:CB] = hi[x * CAP:(x + 1) * CAP]
                parts[i, x, at, CB:2 * CB] = lo[x * CAP:(x + 1) * CAP]
        raw = [lists[pl.ds(j * 16 + h, 8, stride=64), :] for j in range(4)]
        for x in range(NX):
            rows = jnp.zeros((8, GRP), F32)
            for j in range(4):
                rows = jnp.where(lane == j, pltpu.roll(raw[j], ((j - x) % 4) * CAP, 1), rows)
            rows = rows.astype(BF)
            hot = jnp.concatenate(
                [jnp.where(row == rows[g:g + 1, :], one, zero) for g in range(8)], axis=1
            )
            total = jnp.dot(hot, parts[i, x], preferred_element_type=F32)
            out_ref[i, x] = total[:, :CB] + total[:, CB:]


def grads(at, m, c, wt):
    spec = pltpu.PrefetchScalarGridSpec(
        num_scalar_prefetch=1,
        grid=(NZ // 2,),
        in_specs=[
            pl.BlockSpec((NS, 16, TOK), lambda q, at: (0, M_T // 16, 0)),
            pl.BlockSpec((NS, TOK, CB), lambda q, at: (0, 0, 0)),
            pl.BlockSpec((NS, GRP, TOK), lambda q, at: (0, (2 * q - at[0]) & (NZ - 1), 0)),
            pl.BlockSpec((NS, GRP, TOK), lambda q, at: (0, (2 * q + 1 - at[0]) & (NZ - 1), 0)),
        ],
        out_specs=pl.BlockSpec((2, NX, OWN, CB), lambda q, at: (q, 0, 0, 0)),
        scratch_shapes=[
            pltpu.VMEM((2, NX, NS * CAP, 2 * CB), BF),
            pltpu.VMEM((NS * 16, GRP), F32),
        ],
    )
    return pl.pallas_call(
        grads_kernel,
        grid_spec=spec,
        out_shape=jax.ShapeDtypeStruct((NZ, NX, OWN, CB), F32),
        compiler_params=pltpu.CompilerParams(vmem_limit_bytes=56 * MIB),
        cost_estimate=cost(12),
        name="grads",
    )(at, m, c, wt, wt)


EG = 8


def bags_kernel(at_ref, t_ref, wt_ref, v_ref, arrived_ref, out_ref, hots, lists):
    z = at_ref[0]
    for e in range(EG):
        lists[e * 16:(e + 1) * 16, :] = t_ref[e].astype(F32)
    col = lax.broadcasted_iota(jnp.int32, (GRP, OWN), 1).astype(F32)
    for h in range(NZ):
        cols = lists[pl.ds(h, EG, stride=16), :].T
        for e in range(EG):
            hot = jnp.where(col == cols[:, e:e + 1], 1.0, 0.0).astype(BF)
            for x in range(NX):
                hots[x, e * CAP:(e + 1) * CAP, :] = hot[x * CAP:(x + 1) * CAP]
        for x in range(NX):
            rows = v_ref[(z + h) & (NZ - 1), (x - at_ref[1]) & (NX - 1)]
            got = jnp.dot(hots[x], rows, preferred_element_type=F32).astype(BF)
            at = h * GRP + x * CAP
            for e in range(EG):
                arrived_ref[e, at:at + CAP, :] = got[e * CAP:(e + 1) * CAP]
    for e in range(EG):
        bag = lax.dot_general(
            wt_ref[e], arrived_ref[e], (((0,), (0,)), ((), ())), preferred_element_type=F32
        )
        out_ref[e] = bag.astype(BF)


def bags(at, m, wt, v):
    part = lambda g: (g, 0, 0)
    return pl.pallas_call(
        bags_kernel,
        grid=(NS // EG,),
        in_specs=[
            pl.BlockSpec(memory_space=pltpu.SMEM),
            pl.BlockSpec((EG, 16, TOK), lambda g: (g, M_T // 16, 0)),
            pl.BlockSpec((EG, POS, TOK), part),
            pl.BlockSpec((NZ, NX, OWN, CB), lambda g: (0, 0, 0, 0)),
        ],
        out_specs=[pl.BlockSpec((EG, POS, CB), part), pl.BlockSpec((EG, TOK, CB), part)],
        out_shape=[
            jax.ShapeDtypeStruct((NS, POS, CB), BF),
            jax.ShapeDtypeStruct((NS, TOK, CB), BF),
        ],
        scratch_shapes=[
            pltpu.VMEM((NX, EG * CAP, OWN), BF),
            pltpu.VMEM((EG * 16, GRP), F32),
        ],
        compiler_params=pltpu.CompilerParams(vmem_limit_bytes=56 * MIB),
        cost_estimate=cost(18),
        name="bags",
    )(at, m, wt, v)


def scores_kernel(m_ref, c_ref, arrived_ref, out_ref):
    def one(e, carry):
        scores = lax.dot_general(
            c_ref[e], arrived_ref[e], (((1,), (1,)), ((), ())), preferred_element_type=F32
        )
        code = m_ref[e].astype(F32)
        code = jnp.concatenate([code] * (TOK // TOPK), axis=0).T.astype(jnp.int32)
        plane = jnp.zeros_like(code)
        for i in range(1, NZ):
            plane += (code >= (GRP << i)).astype(jnp.int32)
        within = (code >> plane) - GRP
        acc = jnp.zeros((TOK, GRP), F32)
        for h in range(NZ):
            tile = jnp.take_along_axis(
                scores[:, h * GRP:(h + 1) * GRP], within, axis=1, mode="promise_in_bounds"
            )
            acc = jnp.where(plane == h, tile, acc)
        out_ref[e] = acc.T[0:TOPK, :]
        return carry

    lax.fori_loop(0, EG, one, 0, unroll=8)


def scores(m, c, arrived):
    part = lambda g: (g, 0, 0)
    return pl.pallas_call(
        scores_kernel,
        grid=(NS // EG,),
        in_specs=[
            pl.BlockSpec((EG, TOPK, TOK), lambda g: (g, 1, 0)),
            pl.BlockSpec((EG, TOK, CB), part),
            pl.BlockSpec((EG, POS, CB), part),
        ],
        out_specs=pl.BlockSpec((EG, TOPK, TOK), part),
        out_shape=jax.ShapeDtypeStruct((NS, TOPK, TOK), F32),
        compiler_params=pltpu.CompilerParams(vmem_limit_bytes=56 * MIB),
        cost_estimate=cost(18),
        name="scores",
    )(m, c, arrived)


def gather_kernel(b_ref, out_ref):
    for i in range(b_ref.shape[0]):
        out_ref[:, i * CB:(i + 1) * CB] = b_ref[i]


def gather_blocks(b):
    per = 8
    rows = b.shape[1]
    return pl.pallas_call(
        gather_kernel,
        grid=(b.shape[0] // per,),
        in_specs=[pl.BlockSpec((per, rows, CB), lambda g: (g, 0, 0))],
        out_specs=pl.BlockSpec((rows, per * CB), lambda g: (0, g)),
        out_shape=jax.ShapeDtypeStruct((rows, b.shape[0] * CB), b.dtype),
        cost_estimate=cost(2),
        name="rows",
    )(b)


def on_device(slot_weight, slot_pos, touched, values, cotangent):
    x = lax.axis_index("x").astype(jnp.int32)
    d = lax.axis_index("dp").astype(jnp.int32)
    at = jnp.stack([lax.axis_index("z").astype(jnp.int32), x])
    plane = ("dp", "x")
    m = slots(at, slot_weight.T, slot_pos.T, touched)
    m, values, cotangent = lax.optimization_barrier((m, values, cotangent))
    m = lax.all_to_all(m, plane, 0, 0, tiled=True)
    mine = []
    for i in range(NX):
        to = (x - i) & (NX - 1)
        part = lax.dynamic_slice(values, (0, (d * NX + to) * CB), (OWN, CB))
        mine.append(lax.ppermute(part, "x", [(j, (j - i) % NX) for j in range(NX)]) if i else part)
    mine = jnp.stack(mine)
    m, c, _ = lax.optimization_barrier((m, blocks(cotangent), mine))
    v = lax.all_gather(mine, "z")
    c = lax.all_to_all(c, plane, 0, 0, tiled=True)
    wt = dense(m)
    table = grads(at, m, c, wt)
    arrived, b = bags(at, m, wt, v)
    b = lax.all_to_all(b, plane, 0, 0, tiled=True)
    b, g = lax.optimization_barrier((b, scores(m, c, arrived)))
    g = lax.all_to_all(g, plane, 0, 0, tiled=True)
    table = lax.psum_scatter(table, "z", scatter_dimension=0, tiled=True)
    table = lax.all_to_all(table.reshape(NX, OWN, CB), "x", 0, 0, tiled=True)
    value_grad = jnp.concatenate([table[i] for i in range(NX)], axis=1)
    return gather_blocks(b), g.sum(axis=0).T, value_grad


def solution(mesh):
    cube = Mesh(mesh.devices.reshape(ND, NZ, NX), ("dp", "z", "x"))
    tokens = ("dp", "z", "x")
    return jax.shard_map(
        on_device,
        mesh=cube,
        in_specs=(
            P(tokens, None),
            P(tokens, None),
            P(tokens, None, None),
            P(("z", "x"), None),
            P(tokens, None),
        ),
        out_specs=(P(tokens, None), P(tokens, None), P(("z", "x"), "dp")),
        check_vma=False,
    )
```

```python
import jax
import jax.numpy as jnp
from jax import lax
from jax.experimental import pallas as pl
from jax.experimental.pallas import tpu as pltpu
from jax.sharding import Mesh
from jax.sharding import PartitionSpec as P

BF = jnp.bfloat16
F32 = jnp.float32
NZ, NX, ND = 8, 4, 8
NS = ND * NX
TOK = 128
CB = 128
CAP = 32
TOPK = 32
OWN = 256
GRP = NX * CAP
POS = NZ * GRP
M_C = TOPK
M_T = 2 * TOPK
M_V = M_T + 16
PIECE = OWN // ND
M_ALL = M_V + PIECE
MIB = 1024 * 1024


def split(v):
    hi = v.astype(BF)
    return hi, (v - hi.astype(F32)).astype(BF)


def slots_kernel(at_ref, own_ref, w_ref, pos_ref, list_ref, v_ref, out_ref, wide):
    z = at_ref[0]
    pos = pos_ref[...]
    plane = ((pos >> 7) - z) & (NZ - 1)
    code = (((pos & (GRP - 1)) + GRP) << plane).astype(F32).astype(BF)
    lists = list_ref[0]
    owner = lax.broadcasted_iota(jnp.int32, (NX * NZ, GRP), 0) & (NX - 1)
    lane = lax.broadcasted_iota(jnp.int32, (NX * NZ, GRP), 1) // CAP
    wide[...] = jnp.where(owner == lane, jnp.concatenate([lists] * NX, axis=1), 0)
    rows = []
    for h in range(NZ):
        four = [wide[pl.ds(((z + h) & (NZ - 1)) * NX + i, 1), :] for i in range(NX)]
        rows.append(four[0] + four[1] + four[2] + four[3])
    lists = jnp.concatenate(rows + rows, axis=0).astype(F32).astype(BF)
    w = w_ref[...]
    for i in range(NS):
        out_ref[i, 0:M_C, :] = w
        out_ref[i, M_C:M_T, :] = code
        out_ref[i, M_T:M_V, :] = lists
        out_ref[i, M_V:M_ALL, :] = v_ref[:, i * CB:(i + 1) * CB]


def cost(us):
    return pl.CostEstimate(flops=int(us * 1e9), bytes_accessed=2**20, transcendentals=0)


def slots(at, own, w, pos, lists, values):
    spec = pltpu.PrefetchScalarGridSpec(
        num_scalar_prefetch=2,
        grid=(1,),
        in_specs=[
            pl.BlockSpec((TOPK, TOK), lambda i, at, own: (0, 0)),
            pl.BlockSpec((TOPK, TOK), lambda i, at, own: (0, 0)),
            pl.BlockSpec((1, NX * NZ, CAP), lambda i, at, own: (0, 0, 0)),
            pl.BlockSpec((PIECE, NS * CB), lambda i, at, own: (own[0], 0)),
        ],
        out_specs=pl.BlockSpec((NS, M_ALL, TOK), lambda i, at, own: (0, 0, 0)),
        scratch_shapes=[pltpu.VMEM((NX * NZ, GRP), jnp.int32)],
    )
    return pl.pallas_call(
        slots_kernel,
        grid_spec=spec,
        out_shape=jax.ShapeDtypeStruct((NS, M_ALL, TOK), BF),
        compiler_params=pltpu.CompilerParams(vmem_limit_bytes=56 * MIB),
        cost_estimate=cost(2),
        name="slots",
    )(at, own, w, pos, lists, values)


def blocks_kernel(cot_ref, out_ref):
    for i in range(out_ref.shape[0]):
        out_ref[i] = cot_ref[:, i * CB:(i + 1) * CB]


def blocks(cot):
    per = 8
    return pl.pallas_call(
        blocks_kernel,
        grid=(NS // per,),
        in_specs=[pl.BlockSpec((TOK, per * CB), lambda g: (0, g))],
        out_specs=pl.BlockSpec((per, TOK, CB), lambda g: (g, 0, 0)),
        out_shape=jax.ShapeDtypeStruct((NS, TOK, CB), BF),
        cost_estimate=cost(2),
        name="blocks",
    )(cot)


def dense_kernel(m_ref, wt_ref):
    sub = lax.broadcasted_iota(jnp.int32, (GRP, TOK), 0)
    codes = ((sub + GRP) << (2 * pl.program_id(0))).astype(F32).astype(BF)
    tile = 16
    tiles = [codes[i:i + tile] for i in range(0, GRP, tile)]

    def one(e, carry):
        accs = [[jnp.zeros((tile, TOK), BF) for _ in tiles] for _ in range(2)]
        we = m_ref[e, 0:M_C, :]
        ce = m_ref[e, M_C:M_T, :]
        for k in range(TOPK):
            w = jnp.broadcast_to(we[k:k + 1, :], (tile, TOK))
            at = jnp.broadcast_to(ce[k:k + 1, :], (tile, TOK))
            for acc in accs:
                for i, t in enumerate(tiles):
                    acc[i] = jnp.where(t == at, w, acc[i])
                at = at * jnp.asarray(0.5, BF)
        for j, acc in enumerate(accs):
            for i, t in enumerate(acc):
                wt_ref[e, j * GRP + i * tile:j * GRP + (i + 1) * tile, :] = t
        return carry

    lax.fori_loop(0, NS, one, 0, unroll=4)


def dense(m):
    return pl.pallas_call(
        dense_kernel,
        grid=(NZ // 2,),
        in_specs=[pl.BlockSpec((NS, M_T, TOK), lambda h: (0, 0, 0))],
        out_specs=pl.BlockSpec((NS, 2 * GRP, TOK), lambda h: (0, h, 0)),
        out_shape=jax.ShapeDtypeStruct((NS, POS, TOK), BF),
        compiler_params=pltpu.CompilerParams(vmem_limit_bytes=63 * MIB),
        cost_estimate=cost(25),
        name="dense",
    )(m)


def grads_kernel(at_ref, t_ref, c_ref, wt0_ref, wt1_ref, out_ref, parts, lists):
    q = pl.program_id(0)

    @pl.when(q == 0)
    def _():
        for e in range(NS):
            lists[e * 16:(e + 1) * 16, :] = t_ref[e].astype(F32)

    lane = lax.broadcasted_iota(jnp.int32, (8, GRP), 1) // CAP
    row = lax.broadcasted_iota(jnp.int32, (OWN, GRP), 0).astype(F32).astype(BF)
    one, zero = jnp.ones((), BF), jnp.zeros((), BF)
    for i, wt_ref in enumerate((wt0_ref, wt1_ref)):
        h = (2 * q + i - at_ref[0]) & (NZ - 1)
        for e in range(NS):
            hi, lo = split(jnp.dot(wt_ref[e], c_ref[e], preferred_element_type=F32))
            for x in range(NX):
                at = slice(e * CAP, (e + 1) * CAP)
                parts[i, x, at, 0:CB] = hi[x * CAP:(x + 1) * CAP]
                parts[i, x, at, CB:2 * CB] = lo[x * CAP:(x + 1) * CAP]
        raw = [lists[pl.ds(j * 16 + h, 8, stride=64), :] for j in range(4)]
        for x in range(NX):
            rows = jnp.zeros((8, GRP), F32)
            for j in range(4):
                rows = jnp.where(lane == j, pltpu.roll(raw[j], ((j - x) % 4) * CAP, 1), rows)
            rows = rows.astype(BF)
            hot = jnp.concatenate(
                [jnp.where(row == rows[g:g + 1, :], one, zero) for g in range(8)], axis=1
            )
            total = jnp.dot(hot, parts[i, x], preferred_element_type=F32)
            out_ref[i, x] = total[:, :CB] + total[:, CB:]


def grads(at, m, c, wt):
    spec = pltpu.PrefetchScalarGridSpec(
        num_scalar_prefetch=1,
        grid=(NZ // 2,),
        in_specs=[
            pl.BlockSpec((NS, 16, TOK), lambda q, at: (0, M_T // 16, 0)),
            pl.BlockSpec((NS, TOK, CB), lambda q, at: (0, 0, 0)),
            pl.BlockSpec((NS, GRP, TOK), lambda q, at: (0, (2 * q - at[0]) & (NZ - 1), 0)),
            pl.BlockSpec((NS, GRP, TOK), lambda q, at: (0, (2 * q + 1 - at[0]) & (NZ - 1), 0)),
        ],
        out_specs=pl.BlockSpec((2, NX, OWN, CB), lambda q, at: (q, 0, 0, 0)),
        scratch_shapes=[
            pltpu.VMEM((2, NX, NS * CAP, 2 * CB), BF),
            pltpu.VMEM((NS * 16, GRP), F32),
        ],
    )
    return pl.pallas_call(
        grads_kernel,
        grid_spec=spec,
        out_shape=jax.ShapeDtypeStruct((NZ, NX, OWN, CB), F32),
        compiler_params=pltpu.CompilerParams(vmem_limit_bytes=56 * MIB),
        cost_estimate=cost(12),
        name="grads",
    )(at, m, c, wt, wt)


EG = 8


def bags_kernel(at_ref, t_ref, wt_ref, v_ref, arrived_ref, out_ref, hots, lists):
    z = at_ref[0]
    for e in range(EG):
        lists[e * 16:(e + 1) * 16, :] = t_ref[e].astype(F32)
    col = lax.broadcasted_iota(jnp.int32, (GRP, OWN), 1).astype(F32)
    for h in range(NZ):
        cols = lists[pl.ds(h, EG, stride=16), :].T
        for e in range(EG):
            hot = jnp.where(col == cols[:, e:e + 1], 1.0, 0.0).astype(BF)
            for x in range(NX):
                hots[x, e * CAP:(e + 1) * CAP, :] = hot[x * CAP:(x + 1) * CAP]
        for x in range(NX):
            rows = jnp.concatenate(
                [v_ref[(z + h) & (NZ - 1), d * NX + x] for d in range(ND)], axis=0
            )
            got = jnp.dot(hots[x], rows, preferred_element_type=F32).astype(BF)
            at = h * GRP + x * CAP
            for e in range(EG):
                arrived_ref[e, at:at + CAP, :] = got[e * CAP:(e + 1) * CAP]
    for e in range(EG):
        bag = lax.dot_general(
            wt_ref[e], arrived_ref[e], (((0,), (0,)), ((), ())), preferred_element_type=F32
        )
        out_ref[e] = bag.astype(BF)


def bags(at, m, wt, v):
    part = lambda g: (g, 0, 0)
    return pl.pallas_call(
        bags_kernel,
        grid=(NS // EG,),
        in_specs=[
            pl.BlockSpec(memory_space=pltpu.SMEM),
            pl.BlockSpec((EG, 16, TOK), lambda g: (g, M_T // 16, 0)),
            pl.BlockSpec((EG, POS, TOK), part),
            pl.BlockSpec((NZ, NS, PIECE, CB), lambda g: (0, 0, 0, 0)),
        ],
        out_specs=[pl.BlockSpec((EG, POS, CB), part), pl.BlockSpec((EG, TOK, CB), part)],
        out_shape=[
            jax.ShapeDtypeStruct((NS, POS, CB), BF),
            jax.ShapeDtypeStruct((NS, TOK, CB), BF),
        ],
        scratch_shapes=[
            pltpu.VMEM((NX, EG * CAP, OWN), BF),
            pltpu.VMEM((EG * 16, GRP), F32),
        ],
        compiler_params=pltpu.CompilerParams(vmem_limit_bytes=56 * MIB),
        cost_estimate=cost(18),
        name="bags",
    )(at, m, wt, v)


def scores_kernel(m_ref, c_ref, arrived_ref, out_ref):
    def one(e, carry):
        scores = lax.dot_general(
            c_ref[e], arrived_ref[e], (((1,), (1,)), ((), ())), preferred_element_type=F32
        )
        code = m_ref[e].astype(F32)
        code = jnp.concatenate([code] * (TOK // TOPK), axis=0).T.astype(jnp.int32)
        plane = jnp.zeros_like(code)
        for i in range(1, NZ):
            plane += (code >= (GRP << i)).astype(jnp.int32)
        within = (code >> plane) - GRP
        acc = jnp.zeros((TOK, GRP), F32)
        for h in range(NZ):
            tile = jnp.take_along_axis(
                scores[:, h * GRP:(h + 1) * GRP], within, axis=1, mode="promise_in_bounds"
            )
            acc = jnp.where(plane == h, tile, acc)
        out_ref[e] = acc.T[0:TOPK, :]
        return carry

    lax.fori_loop(0, EG, one, 0, unroll=8)


def scores(m, c, arrived):
    part = lambda g: (g, 0, 0)
    return pl.pallas_call(
        scores_kernel,
        grid=(NS // EG,),
        in_specs=[
            pl.BlockSpec((EG, TOPK, TOK), lambda g: (g, 1, 0)),
            pl.BlockSpec((EG, TOK, CB), part),
            pl.BlockSpec((EG, POS, CB), part),
        ],
        out_specs=pl.BlockSpec((EG, TOPK, TOK), part),
        out_shape=jax.ShapeDtypeStruct((NS, TOPK, TOK), F32),
        compiler_params=pltpu.CompilerParams(vmem_limit_bytes=63 * MIB),
        cost_estimate=cost(18),
        name="scores",
    )(m, c, arrived)


def gather_kernel(b_ref, out_ref):
    for i in range(b_ref.shape[0]):
        out_ref[:, i * CB:(i + 1) * CB] = b_ref[i]


def gather_blocks(b):
    per = 8
    rows = b.shape[1]
    return pl.pallas_call(
        gather_kernel,
        grid=(b.shape[0] // per,),
        in_specs=[pl.BlockSpec((per, rows, CB), lambda g: (g, 0, 0))],
        out_specs=pl.BlockSpec((rows, per * CB), lambda g: (0, g)),
        out_shape=jax.ShapeDtypeStruct((rows, b.shape[0] * CB), b.dtype),
        cost_estimate=cost(2),
        name="rows",
    )(b)


def on_device(slot_weight, slot_pos, touched, values, cotangent):
    at = lax.axis_index("z").astype(jnp.int32).reshape(1)
    own = lax.axis_index("dp").astype(jnp.int32).reshape(1)
    plane = ("dp", "x")
    m = slots(at, own, slot_weight.T, slot_pos.T, touched, values)
    m = lax.all_to_all(m, plane, 0, 0, tiled=True)
    m, c = lax.optimization_barrier((m, blocks(cotangent)))
    v = lax.all_gather(m[:, M_V:, :], "z")
    c = lax.all_to_all(c, plane, 0, 0, tiled=True)
    wt = dense(m)
    table = grads(at, m, c, wt)
    arrived, b = bags(at, m, wt, v)
    b = lax.all_to_all(b, plane, 0, 0, tiled=True)
    b, g = lax.optimization_barrier((b, scores(m, c, arrived)))
    g = lax.all_to_all(g, plane, 0, 0, tiled=True)
    table = lax.psum_scatter(table, "z", scatter_dimension=0, tiled=True)
    table = lax.all_to_all(table.reshape(NX, OWN, CB), "x", 0, 0, tiled=True)
    value_grad = jnp.concatenate([table[i] for i in range(NX)], axis=1)
    return gather_blocks(b), g.sum(axis=0).T, value_grad


def solution(mesh):
    cube = Mesh(mesh.devices.reshape(ND, NZ, NX), ("dp", "z", "x"))
    tokens = ("dp", "z", "x")
    return jax.shard_map(
        on_device,
        mesh=cube,
        in_specs=(
            P(tokens, None),
            P(tokens, None),
            P(tokens, None, None),
            P(("z", "x"), None),
            P(tokens, None),
        ),
        out_specs=(P(tokens, None), P(tokens, None), P(("z", "x"), "dp")),
        check_vma=False,
    )
```

```python
import jax
import jax.numpy as jnp
from jax import lax
from jax.experimental import pallas as pl
from jax.experimental.pallas import tpu as pltpu
from jax.sharding import Mesh
from jax.sharding import PartitionSpec as P

BF = jnp.bfloat16
F32 = jnp.float32
NZ, NX, ND = 8, 4, 8
NS = ND * NX
TOK = 128
CB = 128
CAP = 32
TOPK = 32
OWN = 256
GRP = NX * CAP
POS = NZ * GRP
M_C = TOPK
M_V = 2 * TOPK
PIECE = OWN // ND
M_ALL = M_V + PIECE
C_ALL = TOK + 16
MIB = 1024 * 1024


def split(v):
    hi = v.astype(BF)
    return hi, (v - hi.astype(F32)).astype(BF)


def slots_kernel(at_ref, own_ref, w_ref, pos_ref, v_ref, out_ref):
    z = at_ref[0]
    pos = pos_ref[...]
    plane = ((pos >> 7) - z) & (NZ - 1)
    code = (((pos & (GRP - 1)) + GRP) << plane).astype(F32).astype(BF)
    w = w_ref[...]
    for i in range(NS):
        out_ref[i, 0:M_C, :] = w
        out_ref[i, M_C:M_V, :] = code
        out_ref[i, M_V:M_ALL, :] = v_ref[:, i * CB:(i + 1) * CB]


def cost(us):
    return pl.CostEstimate(flops=int(us * 1e9), bytes_accessed=2**20, transcendentals=0)


def slots(at, own, w, pos, values):
    spec = pltpu.PrefetchScalarGridSpec(
        num_scalar_prefetch=2,
        grid=(1,),
        in_specs=[
            pl.BlockSpec((TOPK, TOK), lambda i, at, own: (0, 0)),
            pl.BlockSpec((TOPK, TOK), lambda i, at, own: (0, 0)),
            pl.BlockSpec((PIECE, NS * CB), lambda i, at, own: (own[0], 0)),
        ],
        out_specs=pl.BlockSpec((NS, M_ALL, TOK), lambda i, at, own: (0, 0, 0)),
    )
    return pl.pallas_call(
        slots_kernel,
        grid_spec=spec,
        out_shape=jax.ShapeDtypeStruct((NS, M_ALL, TOK), BF),
        compiler_params=pltpu.CompilerParams(vmem_limit_bytes=56 * MIB),
        cost_estimate=cost(2),
        name="slots",
    )(at, own, w, pos, values)


def blocks_kernel(at_ref, cot_ref, list_ref, out_ref, wide):
    z = at_ref[0]
    lists = list_ref[0]
    owner = lax.broadcasted_iota(jnp.int32, (NX * NZ, GRP), 0) & (NX - 1)
    lane = lax.broadcasted_iota(jnp.int32, (NX * NZ, GRP), 1) // CAP
    wide[...] = jnp.where(owner == lane, jnp.concatenate([lists] * NX, axis=1), 0)
    rows = []
    for h in range(NZ):
        four = [wide[pl.ds(((z + h) & (NZ - 1)) * NX + i, 1), :] for i in range(NX)]
        rows.append(four[0] + four[1] + four[2] + four[3])
    lists = jnp.concatenate(rows + rows, axis=0).astype(F32).astype(BF)
    for i in range(out_ref.shape[0]):
        out_ref[i, 0:TOK, :] = cot_ref[:, i * CB:(i + 1) * CB]
        out_ref[i, TOK:C_ALL, :] = lists


def blocks(at, cot, lists):
    per = 8
    spec = pltpu.PrefetchScalarGridSpec(
        num_scalar_prefetch=1,
        grid=(NS // per,),
        in_specs=[
            pl.BlockSpec((TOK, per * CB), lambda g, at: (0, g)),
            pl.BlockSpec((1, NX * NZ, CAP), lambda g, at: (0, 0, 0)),
        ],
        out_specs=pl.BlockSpec((per, C_ALL, CB), lambda g, at: (g, 0, 0)),
        scratch_shapes=[pltpu.VMEM((NX * NZ, GRP), jnp.int32)],
    )
    return pl.pallas_call(
        blocks_kernel,
        grid_spec=spec,
        out_shape=jax.ShapeDtypeStruct((NS, C_ALL, CB), BF),
        cost_estimate=cost(3),
        name="blocks",
    )(at, cot, lists)


def dense_kernel(m_ref, wt_ref):
    sub = lax.broadcasted_iota(jnp.int32, (GRP, TOK), 0)
    codes = ((sub + GRP) << (2 * pl.program_id(0))).astype(F32).astype(BF)
    tile = 16
    tiles = [codes[i:i + tile] for i in range(0, GRP, tile)]

    def one(e, carry):
        accs = [[jnp.zeros((tile, TOK), BF) for _ in tiles] for _ in range(2)]
        we = m_ref[e, 0:M_C, :]
        ce = m_ref[e, M_C:M_V, :]
        for k in range(TOPK):
            w = jnp.broadcast_to(we[k:k + 1, :], (tile, TOK))
            at = jnp.broadcast_to(ce[k:k + 1, :], (tile, TOK))
            for acc in accs:
                for i, t in enumerate(tiles):
                    acc[i] = jnp.where(t == at, w, acc[i])
                at = at * jnp.asarray(0.5, BF)
        for j, acc in enumerate(accs):
            for i, t in enumerate(acc):
                wt_ref[e, j * GRP + i * tile:j * GRP + (i + 1) * tile, :] = t
        return carry

    lax.fori_loop(0, NS, one, 0, unroll=4)


def dense(m):
    return pl.pallas_call(
        dense_kernel,
        grid=(NZ // 2,),
        in_specs=[pl.BlockSpec((NS, M_V, TOK), lambda h: (0, 0, 0))],
        out_specs=pl.BlockSpec((NS, 2 * GRP, TOK), lambda h: (0, h, 0)),
        out_shape=jax.ShapeDtypeStruct((NS, POS, TOK), BF),
        compiler_params=pltpu.CompilerParams(vmem_limit_bytes=63 * MIB),
        cost_estimate=cost(25),
        name="dense",
    )(m)


def grads_kernel(at_ref, t_ref, c_ref, wt0_ref, wt1_ref, out_ref, parts, lists):
    q = pl.program_id(0)

    @pl.when(q == 0)
    def _():
        for e in range(NS):
            lists[e * 16:(e + 1) * 16, :] = t_ref[e].astype(F32)

    lane = lax.broadcasted_iota(jnp.int32, (8, GRP), 1) // CAP
    row = lax.broadcasted_iota(jnp.int32, (OWN, GRP), 0).astype(F32).astype(BF)
    one, zero = jnp.ones((), BF), jnp.zeros((), BF)
    for i, wt_ref in enumerate((wt0_ref, wt1_ref)):
        h = (2 * q + i - at_ref[0]) & (NZ - 1)
        for e in range(NS):
            hi, lo = split(jnp.dot(wt_ref[e], c_ref[e], preferred_element_type=F32))
            for x in range(NX):
                at = slice(e * CAP, (e + 1) * CAP)
                parts[i, x, at, 0:CB] = hi[x * CAP:(x + 1) * CAP]
                parts[i, x, at, CB:2 * CB] = lo[x * CAP:(x + 1) * CAP]
        raw = [lists[pl.ds(j * 16 + h, 8, stride=64), :] for j in range(4)]
        for x in range(NX):
            rows = jnp.zeros((8, GRP), F32)
            for j in range(4):
                rows = jnp.where(lane == j, pltpu.roll(raw[j], ((j - x) % 4) * CAP, 1), rows)
            rows = rows.astype(BF)
            hot = jnp.concatenate(
                [jnp.where(row == rows[g:g + 1, :], one, zero) for g in range(8)], axis=1
            )
            total = jnp.dot(hot, parts[i, x], preferred_element_type=F32)
            out_ref[i, x] = total[:, :CB] + total[:, CB:]


def grads(at, c, wt):
    spec = pltpu.PrefetchScalarGridSpec(
        num_scalar_prefetch=1,
        grid=(NZ // 2,),
        in_specs=[
            pl.BlockSpec((NS, 16, TOK), lambda q, at: (0, TOK // 16, 0)),
            pl.BlockSpec((NS, TOK, CB), lambda q, at: (0, 0, 0)),
            pl.BlockSpec((NS, GRP, TOK), lambda q, at: (0, (2 * q - at[0]) & (NZ - 1), 0)),
            pl.BlockSpec((NS, GRP, TOK), lambda q, at: (0, (2 * q + 1 - at[0]) & (NZ - 1), 0)),
        ],
        out_specs=pl.BlockSpec((2, NX, OWN, CB), lambda q, at: (q, 0, 0, 0)),
        scratch_shapes=[
            pltpu.VMEM((2, NX, NS * CAP, 2 * CB), BF),
            pltpu.VMEM((NS * 16, GRP), F32),
        ],
    )
    return pl.pallas_call(
        grads_kernel,
        grid_spec=spec,
        out_shape=jax.ShapeDtypeStruct((NZ, NX, OWN, CB), F32),
        compiler_params=pltpu.CompilerParams(vmem_limit_bytes=56 * MIB),
        cost_estimate=cost(12),
        name="grads",
    )(at, c, c, wt, wt)


EG = 8


def bags_kernel(at_ref, t_ref, wt_ref, v_ref, arrived_ref, out_ref, hots, lists):
    z = at_ref[0]
    for e in range(EG):
        lists[e * 16:(e + 1) * 16, :] = t_ref[e].astype(F32)
    col = lax.broadcasted_iota(jnp.int32, (GRP, OWN), 1).astype(F32)
    for h in range(NZ):
        cols = lists[pl.ds(h, EG, stride=16), :].T
        for e in range(EG):
            hot = jnp.where(col == cols[:, e:e + 1], 1.0, 0.0).astype(BF)
            for x in range(NX):
                hots[x, e * CAP:(e + 1) * CAP, :] = hot[x * CAP:(x + 1) * CAP]
        for x in range(NX):
            rows = jnp.concatenate(
                [v_ref[(z + h) & (NZ - 1), d * NX + x] for d in range(ND)], axis=0
            )
            got = jnp.dot(hots[x], rows, preferred_element_type=F32).astype(BF)
            at = h * GRP + x * CAP
            for e in range(EG):
                arrived_ref[e, at:at + CAP, :] = got[e * CAP:(e + 1) * CAP]
    for e in range(EG):
        bag = lax.dot_general(
            wt_ref[e], arrived_ref[e], (((0,), (0,)), ((), ())), preferred_element_type=F32
        )
        out_ref[e] = bag.astype(BF)


def bags(at, c, wt, v):
    part = lambda g: (g, 0, 0)
    return pl.pallas_call(
        bags_kernel,
        grid=(NS // EG,),
        in_specs=[
            pl.BlockSpec(memory_space=pltpu.SMEM),
            pl.BlockSpec((EG, 16, TOK), lambda g: (g, TOK // 16, 0)),
            pl.BlockSpec((EG, POS, TOK), part),
            pl.BlockSpec((NZ, NS, PIECE, CB), lambda g: (0, 0, 0, 0)),
        ],
        out_specs=[pl.BlockSpec((EG, POS, CB), part), pl.BlockSpec((EG, TOK, CB), part)],
        out_shape=[
            jax.ShapeDtypeStruct((NS, POS, CB), BF),
            jax.ShapeDtypeStruct((NS, TOK, CB), BF),
        ],
        scratch_shapes=[
            pltpu.VMEM((NX, EG * CAP, OWN), BF),
            pltpu.VMEM((EG * 16, GRP), F32),
        ],
        compiler_params=pltpu.CompilerParams(vmem_limit_bytes=56 * MIB),
        cost_estimate=cost(18),
        name="bags",
    )(at, c, wt, v)


def scores_kernel(m_ref, c_ref, arrived_ref, out_ref):
    def one(e, carry):
        scores = lax.dot_general(
            c_ref[e], arrived_ref[e], (((1,), (1,)), ((), ())), preferred_element_type=F32
        )
        code = m_ref[e].astype(F32)
        code = jnp.concatenate([code] * (TOK // TOPK), axis=0).T.astype(jnp.int32)
        plane = jnp.zeros_like(code)
        for i in range(1, NZ):
            plane += (code >= (GRP << i)).astype(jnp.int32)
        within = (code >> plane) - GRP
        acc = jnp.zeros((TOK, GRP), F32)
        for h in range(NZ):
            tile = jnp.take_along_axis(
                scores[:, h * GRP:(h + 1) * GRP], within, axis=1, mode="promise_in_bounds"
            )
            acc = jnp.where(plane == h, tile, acc)
        out_ref[e] = acc.T[0:TOPK, :]
        return carry

    lax.fori_loop(0, EG, one, 0, unroll=8)


def scores(m, c, arrived):
    part = lambda g: (g, 0, 0)
    return pl.pallas_call(
        scores_kernel,
        grid=(NS // EG,),
        in_specs=[
            pl.BlockSpec((EG, TOPK, TOK), lambda g: (g, 1, 0)),
            pl.BlockSpec((EG, TOK, CB), part),
            pl.BlockSpec((EG, POS, CB), part),
        ],
        out_specs=pl.BlockSpec((EG, TOPK, TOK), part),
        out_shape=jax.ShapeDtypeStruct((NS, TOPK, TOK), F32),
        compiler_params=pltpu.CompilerParams(vmem_limit_bytes=63 * MIB),
        cost_estimate=cost(18),
        name="scores",
    )(m, c, arrived)


def gather_kernel(b_ref, out_ref):
    for i in range(b_ref.shape[0]):
        out_ref[:, i * CB:(i + 1) * CB] = b_ref[i]


def gather_blocks(b):
    per = 8
    rows = b.shape[1]
    return pl.pallas_call(
        gather_kernel,
        grid=(b.shape[0] // per,),
        in_specs=[pl.BlockSpec((per, rows, CB), lambda g: (g, 0, 0))],
        out_specs=pl.BlockSpec((rows, per * CB), lambda g: (0, g)),
        out_shape=jax.ShapeDtypeStruct((rows, b.shape[0] * CB), b.dtype),
        cost_estimate=cost(2),
        name="rows",
    )(b)


def on_device(slot_weight, slot_pos, touched, values, cotangent):
    at = lax.axis_index("z").astype(jnp.int32).reshape(1)
    own = lax.axis_index("dp").astype(jnp.int32).reshape(1)
    plane = ("dp", "x")
    m = slots(at, own, slot_weight.T, slot_pos.T, values)
    m = lax.all_to_all(m, plane, 0, 0, tiled=True)
    m, c = lax.optimization_barrier((m, blocks(at, cotangent, touched)))
    v = lax.all_gather(m[:, M_V:, :], "z")
    c = lax.all_to_all(c, plane, 0, 0, tiled=True)
    wt = dense(m)
    table = grads(at, c, wt)
    arrived, b = bags(at, c, wt, v)
    b = lax.all_to_all(b, plane, 0, 0, tiled=True)
    b, g = lax.optimization_barrier((b, scores(m, c, arrived)))
    g = lax.all_to_all(g, plane, 0, 0, tiled=True)
    table = lax.psum_scatter(table, "z", scatter_dimension=0, tiled=True)
    table = lax.all_to_all(table.reshape(NX, OWN, CB), "x", 0, 0, tiled=True)
    value_grad = jnp.concatenate([table[i] for i in range(NX)], axis=1)
    return gather_blocks(b), g.sum(axis=0).T, value_grad


def solution(mesh):
    cube = Mesh(mesh.devices.reshape(ND, NZ, NX), ("dp", "z", "x"))
    tokens = ("dp", "z", "x")
    return jax.shard_map(
        on_device,
        mesh=cube,
        in_specs=(
            P(tokens, None),
            P(tokens, None),
            P(tokens, None, None),
            P(("z", "x"), None),
            P(tokens, None),
        ),
        out_specs=(P(tokens, None), P(tokens, None), P(("z", "x"), "dp")),
        check_vma=False,
    )
```

```python
import jax
import jax.numpy as jnp
from jax import lax
from jax.experimental import pallas as pl
from jax.experimental.pallas import tpu as pltpu
from jax.sharding import Mesh
from jax.sharding import PartitionSpec as P

BF = jnp.bfloat16
F32 = jnp.float32
NZ, NX, ND = 8, 4, 8
NS = ND * NX
TOK = 128
CB = 128
CAP = 32
TOPK = 32
OWN = 256
GRP = NX * CAP
POS = NZ * GRP
M_C = TOPK
M_ALL = 2 * TOPK
C_ALL = TOK + 16
MIB = 1024 * 1024


def split(v):
    hi = v.astype(BF)
    return hi, (v - hi.astype(F32)).astype(BF)


def slots_kernel(at_ref, w_ref, pos_ref, out_ref):
    z = at_ref[0]
    pos = pos_ref[...]
    plane = ((pos >> 7) - z) & (NZ - 1)
    code = (((pos & (GRP - 1)) + GRP) << plane).astype(F32).astype(BF)
    w = w_ref[...]
    for i in range(NS):
        out_ref[i, 0:M_C, :] = w
        out_ref[i, M_C:M_ALL, :] = code


def cost(us):
    return pl.CostEstimate(flops=int(us * 1e9), bytes_accessed=2**20, transcendentals=0)


def slots(at, w, pos):
    spec = pltpu.PrefetchScalarGridSpec(
        num_scalar_prefetch=1,
        grid=(1,),
        in_specs=[
            pl.BlockSpec((TOPK, TOK), lambda i, at: (0, 0)),
            pl.BlockSpec((TOPK, TOK), lambda i, at: (0, 0)),
        ],
        out_specs=pl.BlockSpec((NS, M_ALL, TOK), lambda i, at: (0, 0, 0)),
    )
    return pl.pallas_call(
        slots_kernel,
        grid_spec=spec,
        out_shape=jax.ShapeDtypeStruct((NS, M_ALL, TOK), BF),
        compiler_params=pltpu.CompilerParams(vmem_limit_bytes=56 * MIB),
        cost_estimate=cost(2),
        name="slots",
    )(at, w, pos)


def blocks_kernel(at_ref, cot_ref, list_ref, out_ref, wide):
    z = at_ref[0]
    lists = list_ref[0]
    owner = lax.broadcasted_iota(jnp.int32, (NX * NZ, GRP), 0) & (NX - 1)
    lane = lax.broadcasted_iota(jnp.int32, (NX * NZ, GRP), 1) // CAP
    wide[...] = jnp.where(owner == lane, jnp.concatenate([lists] * NX, axis=1), 0)
    rows = []
    for h in range(NZ):
        four = [wide[pl.ds(((z + h) & (NZ - 1)) * NX + i, 1), :] for i in range(NX)]
        rows.append(four[0] + four[1] + four[2] + four[3])
    lists = jnp.concatenate(rows + rows, axis=0).astype(F32).astype(BF)
    for i in range(out_ref.shape[0]):
        out_ref[i, 0:TOK, :] = cot_ref[:, i * CB:(i + 1) * CB]
        out_ref[i, TOK:C_ALL, :] = lists


def blocks(at, cot, lists):
    per = 8
    spec = pltpu.PrefetchScalarGridSpec(
        num_scalar_prefetch=1,
        grid=(NS // per,),
        in_specs=[
            pl.BlockSpec((TOK, per * CB), lambda g, at: (0, g)),
            pl.BlockSpec((1, NX * NZ, CAP), lambda g, at: (0, 0, 0)),
        ],
        out_specs=pl.BlockSpec((per, C_ALL, CB), lambda g, at: (g, 0, 0)),
        scratch_shapes=[pltpu.VMEM((NX * NZ, GRP), jnp.int32)],
    )
    return pl.pallas_call(
        blocks_kernel,
        grid_spec=spec,
        out_shape=jax.ShapeDtypeStruct((NS, C_ALL, CB), BF),
        cost_estimate=cost(3),
        name="blocks",
    )(at, cot, lists)


def dense_kernel(m_ref, wt_ref):
    sub = lax.broadcasted_iota(jnp.int32, (GRP, TOK), 0)
    codes = ((sub + GRP) << (2 * pl.program_id(0))).astype(F32).astype(BF)
    tile = 16
    tiles = [codes[i:i + tile] for i in range(0, GRP, tile)]

    def one(e, carry):
        accs = [[jnp.zeros((tile, TOK), BF) for _ in tiles] for _ in range(2)]
        we = m_ref[e, 0:M_C, :]
        ce = m_ref[e, M_C:M_ALL, :]
        for k in range(TOPK):
            w = jnp.broadcast_to(we[k:k + 1, :], (tile, TOK))
            at = jnp.broadcast_to(ce[k:k + 1, :], (tile, TOK))
            for acc in accs:
                for i, t in enumerate(tiles):
                    acc[i] = jnp.where(t == at, w, acc[i])
                at = at * jnp.asarray(0.5, BF)
        for j, acc in enumerate(accs):
            for i, t in enumerate(acc):
                wt_ref[e, j * GRP + i * tile:j * GRP + (i + 1) * tile, :] = t
        return carry

    lax.fori_loop(0, NS, one, 0, unroll=4)


def dense(m):
    return pl.pallas_call(
        dense_kernel,
        grid=(NZ // 2,),
        in_specs=[pl.BlockSpec((NS, M_ALL, TOK), lambda h: (0, 0, 0))],
        out_specs=pl.BlockSpec((NS, 2 * GRP, TOK), lambda h: (0, h, 0)),
        out_shape=jax.ShapeDtypeStruct((NS, POS, TOK), BF),
        compiler_params=pltpu.CompilerParams(vmem_limit_bytes=63 * MIB),
        cost_estimate=cost(25),
        name="dense",
    )(m)


def grads_kernel(at_ref, t_ref, c_ref, wt0_ref, wt1_ref, out_ref, parts, lists):
    q = pl.program_id(0)

    @pl.when(q == 0)
    def _():
        for e in range(NS):
            lists[e * 16:(e + 1) * 16, :] = t_ref[e].astype(F32)

    lane = lax.broadcasted_iota(jnp.int32, (8, GRP), 1) // CAP
    row = lax.broadcasted_iota(jnp.int32, (OWN, GRP), 0).astype(F32).astype(BF)
    one, zero = jnp.ones((), BF), jnp.zeros((), BF)
    for i, wt_ref in enumerate((wt0_ref, wt1_ref)):
        h = (2 * q + i - at_ref[0]) & (NZ - 1)
        for e in range(NS):
            hi, lo = split(jnp.dot(wt_ref[e], c_ref[e], preferred_element_type=F32))
            for x in range(NX):
                at = slice(e * CAP, (e + 1) * CAP)
                parts[i, x, at, 0:CB] = hi[x * CAP:(x + 1) * CAP]
                parts[i, x, at, CB:2 * CB] = lo[x * CAP:(x + 1) * CAP]
        raw = [lists[pl.ds(j * 16 + h, 8, stride=64), :] for j in range(4)]
        for x in range(NX):
            rows = jnp.zeros((8, GRP), F32)
            for j in range(4):
                rows = jnp.where(lane == j, pltpu.roll(raw[j], ((j - x) % 4) * CAP, 1), rows)
            rows = rows.astype(BF)
            hot = jnp.concatenate(
                [jnp.where(row == rows[g:g + 1, :], one, zero) for g in range(8)], axis=1
            )
            total = jnp.dot(hot, parts[i, x], preferred_element_type=F32)
            out_ref[i, x] = total[:, :CB] + total[:, CB:]


def grads(at, c, wt):
    spec = pltpu.PrefetchScalarGridSpec(
        num_scalar_prefetch=1,
        grid=(NZ // 2,),
        in_specs=[
            pl.BlockSpec((NS, 16, TOK), lambda q, at: (0, TOK // 16, 0)),
            pl.BlockSpec((NS, TOK, CB), lambda q, at: (0, 0, 0)),
            pl.BlockSpec((NS, GRP, TOK), lambda q, at: (0, (2 * q - at[0]) & (NZ - 1), 0)),
            pl.BlockSpec((NS, GRP, TOK), lambda q, at: (0, (2 * q + 1 - at[0]) & (NZ - 1), 0)),
        ],
        out_specs=pl.BlockSpec((2, NX, OWN, CB), lambda q, at: (q, 0, 0, 0)),
        scratch_shapes=[
            pltpu.VMEM((2, NX, NS * CAP, 2 * CB), BF),
            pltpu.VMEM((NS * 16, GRP), F32),
        ],
    )
    return pl.pallas_call(
        grads_kernel,
        grid_spec=spec,
        out_shape=jax.ShapeDtypeStruct((NZ, NX, OWN, CB), F32),
        compiler_params=pltpu.CompilerParams(vmem_limit_bytes=56 * MIB),
        cost_estimate=cost(12),
        name="grads",
    )(at, c, c, wt, wt)


EG = 8


def bags_kernel(at_ref, x_ref, t_ref, wt_ref, v_ref, arrived_ref, out_ref, hots, lists):
    z = at_ref[0]
    for e in range(EG):
        lists[e * 16:(e + 1) * 16, :] = t_ref[e].astype(F32)
    col = lax.broadcasted_iota(jnp.int32, (GRP, OWN), 1).astype(F32)
    for h in range(NZ):
        cols = lists[pl.ds(h, EG, stride=16), :].T
        for e in range(EG):
            hot = jnp.where(col == cols[:, e:e + 1], 1.0, 0.0).astype(BF)
            for x in range(NX):
                hots[x, e * CAP:(e + 1) * CAP, :] = hot[x * CAP:(x + 1) * CAP]
        for x in range(NX):
            rows = v_ref[(z + h) & (NZ - 1), (x - x_ref[0]) & (NX - 1)]
            got = jnp.dot(hots[x], rows, preferred_element_type=F32).astype(BF)
            at = h * GRP + x * CAP
            for e in range(EG):
                arrived_ref[e, at:at + CAP, :] = got[e * CAP:(e + 1) * CAP]
    for e in range(EG):
        bag = lax.dot_general(
            wt_ref[e], arrived_ref[e], (((0,), (0,)), ((), ())), preferred_element_type=F32
        )
        out_ref[e] = bag.astype(BF)


def bags(at, x, c, wt, v):
    part = lambda g: (g, 0, 0)
    return pl.pallas_call(
        bags_kernel,
        grid=(NS // EG,),
        in_specs=[
            pl.BlockSpec(memory_space=pltpu.SMEM),
            pl.BlockSpec(memory_space=pltpu.SMEM),
            pl.BlockSpec((EG, 16, TOK), lambda g: (g, TOK // 16, 0)),
            pl.BlockSpec((EG, POS, TOK), part),
            pl.BlockSpec((NZ, NX, OWN, CB), lambda g: (0, 0, 0, 0)),
        ],
        out_specs=[pl.BlockSpec((EG, POS, CB), part), pl.BlockSpec((EG, TOK, CB), part)],
        out_shape=[
            jax.ShapeDtypeStruct((NS, POS, CB), BF),
            jax.ShapeDtypeStruct((NS, TOK, CB), BF),
        ],
        scratch_shapes=[
            pltpu.VMEM((NX, EG * CAP, OWN), BF),
            pltpu.VMEM((EG * 16, GRP), F32),
        ],
        compiler_params=pltpu.CompilerParams(vmem_limit_bytes=56 * MIB),
        cost_estimate=cost(18),
        name="bags",
    )(at, x, c, wt, v)


def scores_kernel(m_ref, c_ref, arrived_ref, out_ref):
    def one(e, carry):
        scores = lax.dot_general(
            c_ref[e], arrived_ref[e], (((1,), (1,)), ((), ())), preferred_element_type=F32
        )
        code = m_ref[e].astype(F32)
        code = jnp.concatenate([code] * (TOK // TOPK), axis=0).T.astype(jnp.int32)
        plane = jnp.zeros_like(code)
        for i in range(1, NZ):
            plane += (code >= (GRP << i)).astype(jnp.int32)
        within = (code >> plane) - GRP
        acc = jnp.zeros((TOK, GRP), F32)
        for h in range(NZ):
            tile = jnp.take_along_axis(
                scores[:, h * GRP:(h + 1) * GRP], within, axis=1, mode="promise_in_bounds"
            )
            acc = jnp.where(plane == h, tile, acc)
        out_ref[e] = acc.T[0:TOPK, :]
        return carry

    lax.fori_loop(0, EG, one, 0, unroll=8)


def scores(m, c, arrived):
    part = lambda g: (g, 0, 0)
    return pl.pallas_call(
        scores_kernel,
        grid=(NS // EG,),
        in_specs=[
            pl.BlockSpec((EG, TOPK, TOK), lambda g: (g, 1, 0)),
            pl.BlockSpec((EG, TOK, CB), part),
            pl.BlockSpec((EG, POS, CB), part),
        ],
        out_specs=pl.BlockSpec((EG, TOPK, TOK), part),
        out_shape=jax.ShapeDtypeStruct((NS, TOPK, TOK), F32),
        compiler_params=pltpu.CompilerParams(vmem_limit_bytes=63 * MIB),
        cost_estimate=cost(18),
        name="scores",
    )(m, c, arrived)


def gather_kernel(b_ref, out_ref):
    for i in range(b_ref.shape[0]):
        out_ref[:, i * CB:(i + 1) * CB] = b_ref[i]


def gather_blocks(b):
    per = 8
    rows = b.shape[1]
    return pl.pallas_call(
        gather_kernel,
        grid=(b.shape[0] // per,),
        in_specs=[pl.BlockSpec((per, rows, CB), lambda g: (g, 0, 0))],
        out_specs=pl.BlockSpec((rows, per * CB), lambda g: (0, g)),
        out_shape=jax.ShapeDtypeStruct((rows, b.shape[0] * CB), b.dtype),
        cost_estimate=cost(2),
        name="rows",
    )(b)


def on_device(slot_weight, slot_pos, touched, values, cotangent):
    x = lax.axis_index("x").astype(jnp.int32)
    d = lax.axis_index("dp").astype(jnp.int32)
    at = lax.axis_index("z").astype(jnp.int32).reshape(1)
    plane = ("dp", "x")
    parts = []
    for i in range(NX):
        to = (x - i) & (NX - 1)
        parts.append(lax.dynamic_slice(values, (0, (d * NX + to) * CB), (OWN, CB)))
    parts, slot_weight = lax.optimization_barrier((parts, slot_weight))
    mine = parts[:1] + [
        lax.ppermute(parts[i], "x", [(j, (j - i) % NX) for j in range(NX)]) for i in range(1, NX)
    ]
    m = slots(at, slot_weight.T, slot_pos.T)
    m, cotangent, _ = lax.optimization_barrier((m, cotangent, mine[1]))
    m = lax.all_to_all(m, plane, 0, 0, tiled=True)
    mine = jnp.stack(mine)
    m, c, _ = lax.optimization_barrier((m, blocks(at, cotangent, touched), mine))
    v = lax.all_gather(mine, "z")
    c = lax.all_to_all(c, plane, 0, 0, tiled=True)
    wt = dense(m)
    table = grads(at, c, wt)
    arrived, b = bags(at, x.reshape(1), c, wt, v)
    b = lax.all_to_all(b, plane, 0, 0, tiled=True)
    b, g = lax.optimization_barrier((b, scores(m, c, arrived)))
    g = lax.all_to_all(g, plane, 0, 0, tiled=True)
    table = lax.psum_scatter(table, "z", scatter_dimension=0, tiled=True)
    table = lax.all_to_all(table.reshape(NX, OWN, CB), "x", 0, 0, tiled=True)
    value_grad = jnp.concatenate([table[i] for i in range(NX)], axis=1)
    return gather_blocks(b), g.sum(axis=0).T, value_grad


def solution(mesh):
    cube = Mesh(mesh.devices.reshape(ND, NZ, NX), ("dp", "z", "x"))
    tokens = ("dp", "z", "x")
    return jax.shard_map(
        on_device,
        mesh=cube,
        in_specs=(
            P(tokens, None),
            P(tokens, None),
            P(tokens, None, None),
            P(("z", "x"), None),
            P(tokens, None),
        ),
        out_specs=(P(tokens, None), P(tokens, None), P(("z", "x"), "dp")),
        check_vma=False,
    )
```

```python
import jax
import jax.numpy as jnp
from jax import lax
from jax.experimental import pallas as pl
from jax.experimental.pallas import tpu as pltpu
from jax.sharding import Mesh
from jax.sharding import PartitionSpec as P

BF = jnp.bfloat16
F32 = jnp.float32
NZ, NX, ND = 8, 4, 8
NS = ND * NX
TOK = 128
CB = 128
CAP = 32
TOPK = 32
OWN = 256
GRP = NX * CAP
POS = NZ * GRP
M_C = TOPK
M_V = 2 * TOPK
PIECE = OWN // ND
M_ALL = M_V + PIECE
C_ALL = TOK + 16
MIB = 1024 * 1024


def split(v):
    hi = v.astype(BF)
    return hi, (v - hi.astype(F32)).astype(BF)


def columns_of(i):
    return ((i % ND) * NX + i // ND) * CB


def slots_kernel(at_ref, own_ref, w_ref, pos_ref, v_ref, out_ref):
    z = at_ref[0]
    pos = pos_ref[...]
    plane = ((pos >> 7) - z) & (NZ - 1)
    code = (((pos & (GRP - 1)) + GRP) << plane).astype(F32).astype(BF)
    w = w_ref[...]
    for i in range(NS):
        out_ref[i, 0:M_C, :] = w
        out_ref[i, M_C:M_V, :] = code
        out_ref[i, M_V:M_ALL, :] = v_ref[:, columns_of(i):columns_of(i) + CB]


def cost(us):
    return pl.CostEstimate(flops=int(us * 1e9), bytes_accessed=2**20, transcendentals=0)


def slots(at, own, w, pos, values):
    spec = pltpu.PrefetchScalarGridSpec(
        num_scalar_prefetch=2,
        grid=(1,),
        in_specs=[
            pl.BlockSpec((TOPK, TOK), lambda i, at, own: (0, 0)),
            pl.BlockSpec((TOPK, TOK), lambda i, at, own: (0, 0)),
            pl.BlockSpec((PIECE, NS * CB), lambda i, at, own: (own[0], 0)),
        ],
        out_specs=pl.BlockSpec((NS, M_ALL, TOK), lambda i, at, own: (0, 0, 0)),
    )
    return pl.pallas_call(
        slots_kernel,
        grid_spec=spec,
        out_shape=jax.ShapeDtypeStruct((NS, M_ALL, TOK), BF),
        compiler_params=pltpu.CompilerParams(vmem_limit_bytes=56 * MIB),
        cost_estimate=cost(2),
        name="slots",
    )(at, own, w, pos, values)


def blocks_kernel(at_ref, cot_ref, list_ref, out_ref, wide):
    z = at_ref[0]
    lists = list_ref[0]
    owner = lax.broadcasted_iota(jnp.int32, (NX * NZ, GRP), 0) & (NX - 1)
    lane = lax.broadcasted_iota(jnp.int32, (NX * NZ, GRP), 1) // CAP
    wide[...] = jnp.where(owner == lane, jnp.concatenate([lists] * NX, axis=1), 0)
    rows = []
    for h in range(NZ):
        four = [wide[pl.ds(((z + h) & (NZ - 1)) * NX + i, 1), :] for i in range(NX)]
        rows.append(four[0] + four[1] + four[2] + four[3])
    lists = jnp.concatenate(rows + rows, axis=0).astype(F32).astype(BF)
    for i in range(out_ref.shape[0]):
        at = pl.multiple_of((i * NX + pl.program_id(0)) * CB, CB)
        out_ref[i, 0:TOK, :] = cot_ref[:, pl.ds(at, CB)]
        out_ref[i, TOK:C_ALL, :] = lists


def blocks(at, cot, lists):
    per = 8
    spec = pltpu.PrefetchScalarGridSpec(
        num_scalar_prefetch=1,
        grid=(NS // per,),
        in_specs=[
            pl.BlockSpec((TOK, NS * CB), lambda g, at: (0, 0)),
            pl.BlockSpec((1, NX * NZ, CAP), lambda g, at: (0, 0, 0)),
        ],
        out_specs=pl.BlockSpec((per, C_ALL, CB), lambda g, at: (g, 0, 0)),
        scratch_shapes=[pltpu.VMEM((NX * NZ, GRP), jnp.int32)],
    )
    return pl.pallas_call(
        blocks_kernel,
        grid_spec=spec,
        out_shape=jax.ShapeDtypeStruct((NS, C_ALL, CB), BF),
        cost_estimate=cost(3),
        name="blocks",
    )(at, cot, lists)


def dense_kernel(m_ref, wt_ref):
    sub = lax.broadcasted_iota(jnp.int32, (GRP, TOK), 0)
    codes = ((sub + GRP) << (2 * pl.program_id(0))).astype(F32).astype(BF)
    tile = 16
    tiles = [codes[i:i + tile] for i in range(0, GRP, tile)]

    def one(e, carry):
        accs = [[jnp.zeros((tile, TOK), BF) for _ in tiles] for _ in range(2)]
        we = m_ref[e, 0:M_C, :]
        ce = m_ref[e, M_C:M_V, :]
        for k in range(TOPK):
            w = jnp.broadcast_to(we[k:k + 1, :], (tile, TOK))
            at = jnp.broadcast_to(ce[k:k + 1, :], (tile, TOK))
            for acc in accs:
                for i, t in enumerate(tiles):
                    acc[i] = jnp.where(t == at, w, acc[i])
                at = at * jnp.asarray(0.5, BF)
        for j, acc in enumerate(accs):
            for i, t in enumerate(acc):
                wt_ref[e, j * GRP + i * tile:j * GRP + (i + 1) * tile, :] = t
        return carry

    lax.fori_loop(0, NS, one, 0, unroll=4)


def dense(m):
    return pl.pallas_call(
        dense_kernel,
        grid=(NZ // 2,),
        in_specs=[pl.BlockSpec((NS, M_V, TOK), lambda h: (0, 0, 0))],
        out_specs=pl.BlockSpec((NS, 2 * GRP, TOK), lambda h: (0, h, 0)),
        out_shape=jax.ShapeDtypeStruct((NS, POS, TOK), BF),
        compiler_params=pltpu.CompilerParams(vmem_limit_bytes=63 * MIB),
        cost_estimate=cost(25),
        name="dense",
    )(m)


def grads_kernel(at_ref, t_ref, c_ref, wt0_ref, wt1_ref, out_ref, parts, lists):
    q = pl.program_id(0)

    @pl.when(q == 0)
    def _():
        for e in range(NS):
            lists[e * 16:(e + 1) * 16, :] = t_ref[e].astype(F32)

    lane = lax.broadcasted_iota(jnp.int32, (8, GRP), 1) // CAP
    row = lax.broadcasted_iota(jnp.int32, (OWN, GRP), 0).astype(F32).astype(BF)
    one, zero = jnp.ones((), BF), jnp.zeros((), BF)
    for i, wt_ref in enumerate((wt0_ref, wt1_ref)):
        h = (2 * q + i - at_ref[0]) & (NZ - 1)
        for e in range(NS):
            hi, lo = split(jnp.dot(wt_ref[e], c_ref[e], preferred_element_type=F32))
            for x in range(NX):
                at = slice(e * CAP, (e + 1) * CAP)
                parts[i, x, at, 0:CB] = hi[x * CAP:(x + 1) * CAP]
                parts[i, x, at, CB:2 * CB] = lo[x * CAP:(x + 1) * CAP]
        raw = [lists[pl.ds(j * 16 + h, 8, stride=64), :] for j in range(4)]
        for x in range(NX):
            rows = jnp.zeros((8, GRP), F32)
            for j in range(4):
                rows = jnp.where(lane == j, pltpu.roll(raw[j], ((j - x) % 4) * CAP, 1), rows)
            rows = rows.astype(BF)
            hot = jnp.concatenate(
                [jnp.where(row == rows[g:g + 1, :], one, zero) for g in range(8)], axis=1
            )
            total = jnp.dot(hot, parts[i, x], preferred_element_type=F32)
            out_ref[i, x] = total[:, :CB] + total[:, CB:]


def grads(at, c, wt):
    spec = pltpu.PrefetchScalarGridSpec(
        num_scalar_prefetch=1,
        grid=(NZ // 2,),
        in_specs=[
            pl.BlockSpec((NS, 16, TOK), lambda q, at: (0, TOK // 16, 0)),
            pl.BlockSpec((NS, TOK, CB), lambda q, at: (0, 0, 0)),
            pl.BlockSpec((NS, GRP, TOK), lambda q, at: (0, (2 * q - at[0]) & (NZ - 1), 0)),
            pl.BlockSpec((NS, GRP, TOK), lambda q, at: (0, (2 * q + 1 - at[0]) & (NZ - 1), 0)),
        ],
        out_specs=pl.BlockSpec((2, NX, OWN, CB), lambda q, at: (q, 0, 0, 0)),
        scratch_shapes=[
            pltpu.VMEM((2, NX, NS * CAP, 2 * CB), BF),
            pltpu.VMEM((NS * 16, GRP), F32),
        ],
    )
    return pl.pallas_call(
        grads_kernel,
        grid_spec=spec,
        out_shape=jax.ShapeDtypeStruct((NZ, NX, OWN, CB), F32),
        compiler_params=pltpu.CompilerParams(vmem_limit_bytes=56 * MIB),
        cost_estimate=cost(12),
        name="grads",
    )(at, c, c, wt, wt)


EG = 8


def bags_kernel(at_ref, t_ref, wt_ref, v_ref, arrived_ref, out_ref, hots, lists):
    z = at_ref[0]
    for e in range(EG):
        lists[e * 16:(e + 1) * 16, :] = t_ref[e].astype(F32)
    col = lax.broadcasted_iota(jnp.int32, (GRP, OWN), 1).astype(F32)
    for h in range(NZ):
        cols = lists[pl.ds(h, EG, stride=16), :].T
        for e in range(EG):
            hot = jnp.where(col == cols[:, e:e + 1], 1.0, 0.0).astype(BF)
            for x in range(NX):
                hots[x, e * CAP:(e + 1) * CAP, :] = hot[x * CAP:(x + 1) * CAP]
        for x in range(NX):
            rows = jnp.concatenate(
                [v_ref[(z + h) & (NZ - 1), x * ND + d] for d in range(ND)], axis=0
            )
            got = jnp.dot(hots[x], rows, preferred_element_type=F32).astype(BF)
            at = h * GRP + x * CAP
            for e in range(EG):
                arrived_ref[e, at:at + CAP, :] = got[e * CAP:(e + 1) * CAP]
    for e in range(EG):
        bag = lax.dot_general(
            wt_ref[e], arrived_ref[e], (((0,), (0,)), ((), ())), preferred_element_type=F32
        )
        out_ref[e] = bag.astype(BF)


def bags(at, c, wt, v):
    part = lambda g: (g, 0, 0)
    return pl.pallas_call(
        bags_kernel,
        grid=(NS // EG,),
        in_specs=[
            pl.BlockSpec(memory_space=pltpu.SMEM),
            pl.BlockSpec((EG, 16, TOK), lambda g: (g, TOK // 16, 0)),
            pl.BlockSpec((EG, POS, TOK), part),
            pl.BlockSpec((NZ, NS, PIECE, CB), lambda g: (0, 0, 0, 0)),
        ],
        out_specs=[pl.BlockSpec((EG, POS, CB), part), pl.BlockSpec((EG, TOK, CB), part)],
        out_shape=[
            jax.ShapeDtypeStruct((NS, POS, CB), BF),
            jax.ShapeDtypeStruct((NS, TOK, CB), BF),
        ],
        scratch_shapes=[
            pltpu.VMEM((NX, EG * CAP, OWN), BF),
            pltpu.VMEM((EG * 16, GRP), F32),
        ],
        compiler_params=pltpu.CompilerParams(vmem_limit_bytes=56 * MIB),
        cost_estimate=cost(18),
        name="bags",
    )(at, c, wt, v)


def scores_kernel(m_ref, c_ref, arrived_ref, out_ref):
    def one(e, carry):
        scores = lax.dot_general(
            c_ref[e], arrived_ref[e], (((1,), (1,)), ((), ())), preferred_element_type=F32
        )
        code = m_ref[e].astype(F32)
        code = jnp.concatenate([code] * (TOK // TOPK), axis=0).T.astype(jnp.int32)
        plane = jnp.zeros_like(code)
        for i in range(1, NZ):
            plane += (code >= (GRP << i)).astype(jnp.int32)
        within = (code >> plane) - GRP
        acc = jnp.zeros((TOK, GRP), F32)
        for h in range(NZ):
            tile = jnp.take_along_axis(
                scores[:, h * GRP:(h + 1) * GRP], within, axis=1, mode="promise_in_bounds"
            )
            acc = jnp.where(plane == h, tile, acc)
        out_ref[e] = acc.T[0:TOPK, :]
        return carry

    lax.fori_loop(0, EG, one, 0, unroll=8)


def scores(m, c, arrived):
    part = lambda g: (g, 0, 0)
    return pl.pallas_call(
        scores_kernel,
        grid=(NS // EG,),
        in_specs=[
            pl.BlockSpec((EG, TOPK, TOK), lambda g: (g, 1, 0)),
            pl.BlockSpec((EG, TOK, CB), part),
            pl.BlockSpec((EG, POS, CB), part),
        ],
        out_specs=pl.BlockSpec((EG, TOPK, TOK), part),
        out_shape=jax.ShapeDtypeStruct((NS, TOPK, TOK), F32),
        compiler_params=pltpu.CompilerParams(vmem_limit_bytes=63 * MIB),
        cost_estimate=cost(18),
        name="scores",
    )(m, c, arrived)


def gather_kernel(b_ref, out_ref):
    for i in range(b_ref.shape[0]):
        out_ref[:, columns_of(i):columns_of(i) + CB] = b_ref[i]


def gather_blocks(b):
    vm = pl.BlockSpec(memory_space=pltpu.VMEM)
    return pl.pallas_call(
        gather_kernel,
        in_specs=[vm],
        out_specs=vm,
        out_shape=jax.ShapeDtypeStruct((TOK, NS * CB), b.dtype),
        cost_estimate=cost(2),
        name="rows",
    )(b)


def on_device(slot_weight, slot_pos, touched, values, cotangent):
    at = lax.axis_index("z").astype(jnp.int32).reshape(1)
    own = lax.axis_index("dp").astype(jnp.int32).reshape(1)
    plane = ("x", "dp")
    m = slots(at, own, slot_weight.T, slot_pos.T, values)
    m = lax.all_to_all(m, plane, 0, 0, tiled=True)
    m, c = lax.optimization_barrier((m, blocks(at, cotangent, touched)))
    v = lax.all_gather(m[:, M_V:, :], "z")
    c = lax.all_to_all(c, plane, 0, 0, tiled=True)
    wt = dense(m)
    table = grads(at, c, wt)
    arrived, b = bags(at, c, wt, v)
    b = lax.all_to_all(b, plane, 0, 0, tiled=True)
    b, g = lax.optimization_barrier((b, scores(m, c, arrived)))
    g = lax.all_to_all(g, plane, 0, 0, tiled=True)
    table = lax.psum_scatter(table, "z", scatter_dimension=0, tiled=True)
    table = lax.all_to_all(table.reshape(NX, OWN, CB), "x", 0, 0, tiled=True)
    value_grad = jnp.concatenate([table[i] for i in range(NX)], axis=1)
    return gather_blocks(b), g.sum(axis=0).T, value_grad


def solution(mesh):
    cube = Mesh(mesh.devices.reshape(ND, NZ, NX), ("dp", "z", "x"))
    tokens = ("dp", "z", "x")
    return jax.shard_map(
        on_device,
        mesh=cube,
        in_specs=(
            P(tokens, None),
            P(tokens, None),
            P(tokens, None, None),
            P(("z", "x"), None),
            P(tokens, None),
        ),
        out_specs=(P(tokens, None), P(tokens, None), P(("z", "x"), "dp")),
        check_vma=False,
    )
```
